32 devices in a mesh: dp: 4 (over y, x), expert: 4 (over z), tensor: 2 (over core).
Axes of the slice: x: 2, y: 2, z: 4, core: 2. Of those that a mesh axis runs over, the one named last changes fastest.
Arguments:
- tokens: bfloat16 [2048, 4096], P(('dp', 'expert')), may hold values from -6 to 6
- cotangent: bfloat16 [2048, 4096], P(('dp', 'expert')), may hold values from -6 to 6
- routes: int32 [2048, 1], P(('dp', 'expert')), may hold values from 0 to 3; in each aligned block of 128 rows (0 to 127, 128 to 255, ...) at most 48 rows name the same one
- cluster: int32 [4, 512], replicated, may hold values from -1 to 1847, as said below
- w_gate: bfloat16 [1848, 4096], P(('expert', 'tensor'), 'dp'), may hold values from -0.09375 to 0.09375
- w_up: bfloat16 [1848, 4096], P(('expert', 'tensor'), 'dp'), may hold values from -0.09375 to 0.09375
- w_down: bfloat16 [1848, 4096], P(('expert', 'tensor'), 'dp'), may hold values from -0.25 to 0.25
Outputs:
- layer_out: bfloat16 [2048, 4096], P(('dp', 'expert'))
- grad_tokens: bfloat16 [2048, 4096], P(('dp', 'expert'))
The draws below stay inside these ranges and needn't reach their ends.
Inputs may be any that keep to these rules, and one draw needn't show every extreme that they name: `routes`: in each aligned block of 128 rows no expert is named more than 48 times, and some block names one expert exactly 48 times; every expert is named somewhere. `cluster`: every neuron appears exactly once and each expert has 462 live slots. Slot j = q * 256 + s * 32 + k (k below 32) holds -1 or a neuron of source shard s, that is a row from s * 231 to (s + 1) * 231 - 1; shard s fills exactly 32 such slots of some experts' halves and fewer of others.
All inputs are finite; a program needn't handle non-finite values.
Results may differ from the reference program's by a relative error of at most 0.0059.
Values may be sent and summed in bfloat16 or wider, within the bound.
No kernel may reach another device: no remote copies, remote signals or barrier semaphores. Data moves between devices by JAX's collectives and lax.ppermute only.
A program may use at most 128 MiB of HBM per device.

```python
import math
import jax
import jax.numpy as jnp
import numpy as np
from jax import lax

D = 4096
LIVE = 462
SLOTS = 512
TOK_DEV = 128
EXPERTS = 4
FFW = 1848
CAP = 48
TOKENS = 2048
N_DP = 4
N_EXPERT = 4
N_TENSOR = 2


def draw_cluster(key, part):
    shards = N_EXPERT * N_TENSOR
    half_slots = SLOTS // N_TENSOR
    per_shard = half_slots // shards
    live_half = LIVE // N_TENSOR
    offset = jax.random.randint(jax.random.fold_in(key, 11), (), 0, half_slots)
    dest = jnp.arange(shards, dtype=jnp.int32)[:, None, None]
    source = jnp.arange(shards, dtype=jnp.int32)[None, :, None]
    within = jnp.arange(per_shard, dtype=jnp.int32)[None, None, :]
    place = (per_shard * (dest + source) + within + offset) % half_slots
    keys = jax.random.split(jax.random.fold_in(key, 23), shards)
    orders = jax.vmap(lambda single: jax.random.permutation(single, live_half))(keys).astype(jnp.int32)
    source_full = jnp.broadcast_to(source, place.shape)
    clipped = jnp.minimum(place, live_half - 1)
    neuron = source_full * live_half + orders[source_full, clipped]
    chosen = jnp.where(place < live_half, neuron, -1)
    return chosen.reshape(N_EXPERT, SLOTS).astype(jnp.int32)


def level_of(rng, extent, pieces, least, top_value):
    def one(axis_at, blocks):
        steps = jax.random.uniform(jax.random.fold_in(jax.random.fold_in(rng, 6), axis_at), (blocks,), jnp.float32, least / len(pieces), top_value / len(pieces))
        return jnp.repeat(jnp.exp(steps), extent[axis_at] // blocks).reshape((-1,) + (1,) * (len(extent) - axis_at - 1))

    level = one(*pieces[0])
    for cut in pieces[1:]:
        level = level * one(*cut)
    return level


def shared_out(key, own, number, rows, count, top, most, slope):
    sequence = jax.random.permutation(key, count)
    crowded, ordinary = shares(count, rows * top, most, slope, True), shares(count, rows * top, most, slope, False)
    places = jnp.arange(count)

    def named(sizes, rotation):
        used = int((sizes > 0).sum())
        fixed = max(1, used // 4)
        shifted = fixed + (places - fixed + rotation * (used - fixed)) % max(1, count - fixed)
        return jnp.zeros((count,), jnp.int32).at[sequence[jnp.where(places < fixed, places, shifted)]].set(jnp.asarray(sizes, jnp.int32))

    sizes = jnp.where(number % 4 == 0, named(crowded, number // 4), named(ordinary, number - number // 4 - 1))
    mixed = jax.random.permutation(jax.random.fold_in(own, 3), count)
    giver, receiver = mixed[0:count // 2 * 2:2], mixed[1:count // 2 * 2:2]
    room = jnp.minimum(sizes[giver] - 1, most - sizes[receiver]) // 2
    room = jnp.where((giver == sequence[0]) | (receiver == sequence[0]) | (sizes[receiver] == 0), 0, jnp.maximum(room, 0))
    shifted = jax.random.randint(jax.random.fold_in(own, 4), (count // 2,), 0, 1 << 20) % (room + 1)
    sizes = sizes.at[giver].add(-shifted).at[receiver].add(shifted)
    labels = jnp.searchsorted(jnp.cumsum(sizes), jnp.arange(rows * top), side="right").astype(jnp.int32)
    listing = labels.reshape(top, rows).T
    listing = listing[jax.random.permutation(jax.random.fold_in(own, 1), rows)]
    rotation = jax.random.randint(jax.random.fold_in(own, 2), (rows, 1), 0, top)
    return jnp.take_along_axis(listing, (jnp.arange(top)[None, :] + rotation) % top, axis=1)


def shares(number_of, total, reach, lean, full):
    loads = [(1 << 20) // math.isqrt(standing ** lean) + 1 for standing in range(1, number_of + 1)]
    largest = reach if full else min(reach, max(-(-total // number_of), total * loads[0] // sum(loads)))
    least = 1 if total - largest >= number_of - 1 else 0
    holding, surplus = [largest] + [least] * (number_of - 1), total - largest - least * (number_of - 1)
    while surplus > 0:
        free = [i for i in range(1, number_of) if holding[i] < largest] or [i for i in range(1, number_of) if holding[i] < reach]
        mass, left = sum([loads[i] for i in free]), surplus
        for i in free:
            addition = min(reach - holding[i], max(1, left * loads[i] // mass), surplus)
            holding[i] = holding[i] + addition
            surplus = surplus - addition
    return np.array(holding)


def centred(stream_key, extent, width, bound, cuts=(), kind=jnp.bfloat16):
    result = width * jax.random.normal(stream_key, extent, jnp.float32)
    if cuts:
        result = result * level_of(stream_key, extent, cuts, -0.22, 0.18)
    return jnp.clip(result, -bound, bound).astype(kind)


def setup_inputs(seed: int = 0) -> dict:
    key_of = jax.random.split(jax.random.key(seed), 8)
    tokens = centred(key_of[0], (TOKENS, D), 1.0, 6.0, ((0, 16),))
    cotangent = centred(key_of[1], (TOKENS, D), 1.0, 6.0, ((0, 16),))
    routes_keys = jax.random.split(jax.random.fold_in(key_of[2], 1), TOKENS // TOK_DEV)
    routes_turns = jax.random.permutation(jax.random.fold_in(key_of[2], 3), TOKENS // TOK_DEV)
    routes = jax.vmap(lambda own, number: shared_out(jax.random.fold_in(key_of[2], 2), own, number, TOK_DEV, EXPERTS, 1, CAP, 2))(routes_keys, routes_turns).reshape((TOKENS, 1))
    cluster = draw_cluster(jax.random.fold_in(key_of[7], 71), 0)
    w_gate = centred(key_of[4], (FFW, D), D ** -0.5, 0.09375, ((0, 8), (1, 4)))
    w_up = centred(key_of[5], (FFW, D), D ** -0.5, 0.09375, ((0, 8), (1, 4)))
    w_down = centred(key_of[6], (FFW, D), LIVE ** -0.5, 0.25, ((0, 8), (1, 4)))
    return {"tokens": tokens, "cotangent": cotangent, "routes": routes, "cluster": cluster, "w_gate": w_gate, "w_up": w_up, "w_down": w_down}


def expert_pass(x_rows, dy_rows, picks, w_gate, w_up, w_down):
    is_live = (picks >= 0)[:, None]
    safe_rows = jnp.clip(picks, 0, w_gate.shape[0] - 1).astype(jnp.int32)
    zero_row = jnp.zeros((), w_gate.dtype)
    gate_rows = jnp.where(is_live, w_gate[safe_rows], zero_row)
    up_rows = jnp.where(is_live, w_up[safe_rows], zero_row)
    down_rows = jnp.where(is_live, w_down[safe_rows], zero_row)
    half_slots = picks.shape[0] // N_TENSOR
    out_sum = jnp.zeros((x_rows.shape[0], x_rows.shape[1]), jnp.float32)
    grad_sum = jnp.zeros((x_rows.shape[0], x_rows.shape[1]), jnp.float32)
    for quarter in range(N_TENSOR):
        lower = quarter * half_slots
        gate_w = gate_rows[lower:lower + half_slots]
        up_w = up_rows[lower:lower + half_slots]
        down_w = down_rows[lower:lower + half_slots]
        pre_gate = jnp.dot(x_rows, gate_w.T, preferred_element_type=jnp.float32)
        pre_up = jnp.dot(x_rows, up_w.T, preferred_element_type=jnp.float32)
        sig_gate = jax.nn.sigmoid(pre_gate)
        hidden = (pre_gate * sig_gate * pre_up).astype(jnp.bfloat16)
        out_part = jnp.dot(hidden, down_w, preferred_element_type=jnp.float32).astype(jnp.bfloat16)
        out_part = lax.optimization_barrier(out_part)
        out_sum = out_sum + out_part.astype(jnp.float32)
        grad_hidden = jnp.dot(dy_rows, down_w.T, preferred_element_type=jnp.float32)
        grad_gate = (grad_hidden * pre_up * sig_gate * (1.0 + pre_gate * (1.0 - sig_gate))).astype(jnp.bfloat16)
        grad_up = (grad_hidden * pre_gate * sig_gate).astype(jnp.bfloat16)
        grad_part = jnp.dot(grad_gate, gate_w, preferred_element_type=jnp.float32)
        grad_part = grad_part + jnp.dot(grad_up, up_w, preferred_element_type=jnp.float32)
        grad_part = lax.optimization_barrier(grad_part.astype(jnp.bfloat16))
        grad_sum = grad_sum + grad_part.astype(jnp.float32)
    return out_sum.astype(jnp.bfloat16), grad_sum.astype(jnp.bfloat16)


def reference(tokens, cotangent, routes, cluster, w_gate, w_up, w_down):
    blocks = N_DP * N_EXPERT
    expert_of = routes[:, 0].reshape(blocks, TOK_DEV)
    onehot = (expert_of[:, :, None] == jnp.arange(N_EXPERT, dtype=jnp.int32)[None, None, :]).astype(jnp.int32)
    position = jnp.sum((jnp.cumsum(onehot, axis=1) - 1) * onehot, axis=2)
    block_ids = jnp.arange(blocks, dtype=jnp.int32)[:, None]
    row_ids = (block_ids * CAP + position).reshape(-1).astype(jnp.int32)
    flat_expert = expert_of.reshape(-1).astype(jnp.int32)
    empty = jnp.zeros((N_EXPERT, blocks * CAP, D), jnp.bfloat16)
    x_buffer = empty.at[flat_expert, row_ids].set(tokens)
    dy_buffer = empty.at[flat_expert, row_ids].set(cotangent)

    def one_expert(items):
        return expert_pass(items[0], items[1], items[2], w_gate, w_up, w_down)

    out_buffer, grad_buffer = lax.map(one_expert, (x_buffer, dy_buffer, cluster))
    layer_out = out_buffer[flat_expert, row_ids]
    grad_tokens = grad_buffer[flat_expert, row_ids]
    return (layer_out, grad_tokens)
```

```python
import functools

import jax
import jax.numpy as jnp
from jax import lax
from jax.experimental import pallas as pl
from jax.experimental.pallas import tpu as pltpu
from jax.sharding import PartitionSpec as P

BF16 = jnp.bfloat16
F32 = jnp.float32
LAST = (((1,), (1,)), ((), ()))
FIRST = (((0,), (0,)), ((), ()))
VMEM_LIMIT = 48 * 1024 * 1024


def flips(size, step):
    return [(i, i ^ step) for i in range(size)]


def select_kernel(n_experts, halves, shards, cluster_ref, gate_ref, up_ref, down_ref, *out_refs):
    mine = lax.axis_index("expert")
    source = mine * halves + lax.axis_index("tensor")
    slots = cluster_ref.shape[1]
    rows = gate_ref.shape[0]
    half = slots // halves
    run = half // shards
    wide = n_experts * halves * run
    lane = lax.broadcasted_iota(jnp.int32, (8, slots), 1)
    picks = jnp.full((8, slots), -1, jnp.int32)
    for k in range(n_experts):
        row = cluster_ref[pl.ds(mine ^ k, 1), :]
        row = jnp.broadcast_to(row, (8, slots))
        for q in range(halves):
            start = (k * halves + q) * run
            shift = lax.rem(start + 2 * slots - q * half - source * run, slots)
            moved = pltpu.roll(row, shift, 1)
            picks = jnp.where((lane >= start) & (lane < start + run), moved, picks)
    local = jnp.where(picks >= 0, picks - source * rows, -1)[0:1, :wide]
    neuron = lax.broadcasted_iota(jnp.int32, (rows, wide), 0)
    table = jnp.where(neuron == local, 1.0, 0.0).astype(BF16)
    per = halves * run
    for w, ref in enumerate((gate_ref, up_ref, down_ref)):
        chosen = lax.dot_general(table, ref[...], FIRST, preferred_element_type=F32).astype(BF16)
        for k in range(n_experts):
            out_refs[k][w * per:(w + 1) * per, :] = chosen[k * per:(k + 1) * per]


def slot_table(routes, n_experts, capacity):
    tokens = routes.shape[1]
    across = jnp.broadcast_to(routes, (tokens, tokens))
    down = jnp.transpose(across)
    i = lax.broadcasted_iota(jnp.int32, (tokens, tokens), 0)
    j = lax.broadcasted_iota(jnp.int32, (tokens, tokens), 1)
    before = jnp.where((across == down) & (i < j), 1, 0)
    position = jnp.sum(before, axis=0, keepdims=True)
    slot = (routes ^ lax.axis_index("expert")) * capacity + position
    number = lax.broadcasted_iota(jnp.int32, (n_experts * capacity, tokens), 0)
    return jnp.where(number == slot, 1.0, 0.0).astype(BF16)


def dispatch_kernel(n_experts, capacity, routes_ref, tokens_ref, cotangent_ref, *refs):
    out_refs, table_ref = refs[:-1], refs[-1]

    @pl.when(pl.program_id(0) == 0)
    def _():
        table_ref[...] = slot_table(routes_ref[...], n_experts, capacity)

    def send(source_ref):
        sent = jnp.dot(table_ref[...], source_ref[...], preferred_element_type=F32).astype(BF16)
        for k in range(n_experts):
            out_refs[k][...] = sent[k * capacity:(k + 1) * capacity]

    core = lax.axis_index("tensor")
    pl.when(core == 0)(lambda: send(tokens_ref))
    pl.when(core != 0)(lambda: send(cotangent_ref))


def merge_kernel(n_experts, capacity, routes_ref, *refs):
    mine_refs, other_refs = refs[:n_experts], refs[n_experts:2 * n_experts]
    out_ref, grad_ref, table_ref = refs[2 * n_experts:]

    @pl.when(pl.program_id(0) == 0)
    def _():
        table_ref[...] = slot_table(routes_ref[...], n_experts, capacity)

    def home(parts):
        rows = jnp.concatenate([part[...] for part in parts], axis=0)
        return lax.dot_general(table_ref[...], rows, FIRST, preferred_element_type=F32).astype(BF16)

    def both(first, second):
        out_ref[...] = home(first)
        grad_ref[...] = home(second)

    core = lax.axis_index("tensor")
    pl.when(core == 0)(lambda: both(mine_refs, other_refs))
    pl.when(core != 0)(lambda: both(other_refs, mine_refs))


def expert_kernel(n_experts, n_dp, members, capacity, *refs):
    n_parts = n_dp + 1
    n_rows = len(members)
    refs = list(refs)
    weights = [[refs.pop(0) for _ in range(n_parts)] for _ in range(n_experts)]
    mine_refs = [refs.pop(0) for _ in range(n_rows)]
    other_refs = [refs.pop(0) for _ in range(n_rows)]
    keep_refs = [refs.pop(0) for _ in range(n_rows)]
    give_refs = [refs.pop(0) for _ in range(n_rows)]
    w_ref, x_ref, dy_ref, w_sem, row_sem = refs
    me = lax.axis_index("dp")
    core = lax.axis_index("tensor")
    deep, width = w_ref.shape[2], w_ref.shape[3]
    per = deep // 3

    def weight_copies(j):
        copies = []
        for k in range(n_experts):
            if j < n_dp - 1:
                pairs = [(weights[k][j], w_ref.at[k, j], j)]
            else:
                cut = deep // 2
                pairs = [
                    (weights[k][j], w_ref.at[k, j, pl.ds(0, cut)], j),
                    (weights[k][j + 1], w_ref.at[k, j, pl.ds(cut, cut)], j + 1),
                ]
            copies += [pltpu.make_async_copy(a, b, w_sem.at[k, s]) for a, b, s in pairs]
        return copies

    def row_copies(first, second):
        copies = []
        for i in range(n_rows):
            at = pl.ds(i * capacity, capacity)
            copies.append(pltpu.make_async_copy(first[i], x_ref.at[at], row_sem.at[0, i]))
            copies.append(pltpu.make_async_copy(second[i], dy_ref.at[at], row_sem.at[1, i]))
        return copies

    def start(copies):
        for copy in copies:
            copy.start()

    pl.when(core == 0)(lambda: start(row_copies(mine_refs, other_refs)))
    pl.when(core != 0)(lambda: start(row_copies(other_refs, mine_refs)))
    for j in range(n_dp):
        start(weight_copies(j))
    for copy in row_copies(mine_refs, other_refs):
        copy.wait()

    def columns(j):
        return pl.ds(pl.multiple_of((me ^ j) * width, width), width)

    def kind(j, w):
        return jnp.concatenate([w_ref[k, j, w * per:(w + 1) * per, :] for k in range(n_experts)], axis=0)

    pre_gate = pre_up = grad_hidden = 0.0
    for j in range(n_dp):
        for copy in weight_copies(j):
            copy.wait()
        x = x_ref[:, columns(j)]
        dy = dy_ref[:, columns(j)]
        pre_gate += lax.dot_general(x, kind(j, 0), LAST, preferred_element_type=F32)
        pre_up += lax.dot_general(x, kind(j, 1), LAST, preferred_element_type=F32)
        grad_hidden += lax.dot_general(dy, kind(j, 2), LAST, preferred_element_type=F32)
    sig = jax.nn.sigmoid(pre_gate)
    hidden = (pre_gate * sig * pre_up).astype(BF16)
    grad_gate = (grad_hidden * pre_up * sig * (1.0 + pre_gate * (1.0 - sig))).astype(BF16)
    grad_up = (grad_hidden * pre_gate * sig).astype(BF16)
    for j in range(n_dp):
        out = jnp.dot(hidden, kind(j, 2), preferred_element_type=F32).astype(BF16)
        grad = jnp.dot(grad_gate, kind(j, 0), preferred_element_type=F32)
        grad = (grad + jnp.dot(grad_up, kind(j, 1), preferred_element_type=F32)).astype(BF16)

        def store(kept, given):
            for i in range(n_rows):
                at = slice(i * capacity, (i + 1) * capacity)
                keep_refs[i][:, columns(j)] = kept[at]
                give_refs[i][:, columns(j)] = given[at]

        pl.when(core == 0)(lambda: store(out, grad))
        pl.when(core != 0)(lambda: store(grad, out))


def aligned_plan(tokens, cotangent, routes, cluster, w_gate, w_up, w_down):
    n_dp = lax.axis_size("dp")
    n_experts = lax.axis_size("expert")
    halves = lax.axis_size("tensor")
    shards = n_experts * halves
    width_part = w_gate.shape[1]
    tok_count, width = tokens.shape
    run = cluster.shape[1] // (halves * shards)
    per = halves * run
    capacity = 3 * tok_count // (2 * n_experts)
    params = pltpu.CompilerParams(vmem_limit_bytes=VMEM_LIMIT)
    vmem = pl.BlockSpec(memory_space=pltpu.VMEM)
    anywhere = pl.BlockSpec(memory_space=pl.ANY)
    shape = jax.ShapeDtypeStruct

    sent_w = pl.pallas_call(
        functools.partial(select_kernel, n_experts, halves, shards),
        out_shape=[shape((3 * per, width_part), BF16)] * n_experts,
        in_specs=[vmem] * 4,
        out_specs=[vmem] * n_experts,
        compiler_params=params,
        name="select_rows",
    )(cluster, w_gate, w_up, w_down)

    def over_dp(chunk):
        cut = chunk.shape[0] // 2
        near = lax.ppermute(chunk, "dp", flips(n_dp, 1))
        far = lax.ppermute(chunk, "dp", flips(n_dp, 2))
        low = lax.ppermute(near[:cut], "dp", flips(n_dp, 2))
        high = lax.ppermute(far[cut:], "dp", flips(n_dp, 1))
        return [chunk, near, far, low, high]

    weights = [None] * n_experts
    weights[0] = over_dp(sent_w[0])
    for k in (2, 1, 3):
        weights[k] = over_dp(lax.ppermute(sent_w[k], "expert", flips(n_experts, k)))

    route_row = routes.reshape(1, tok_count)
    block = width // 4
    sent = pl.pallas_call(
        functools.partial(dispatch_kernel, n_experts, capacity),
        grid=(width // block,),
        out_shape=[shape((capacity, width), BF16)] * n_experts,
        in_specs=[
            pl.BlockSpec((1, tok_count), lambda i: (0, 0)),
            pl.BlockSpec((tok_count, block), lambda i: (0, i)),
            pl.BlockSpec((tok_count, block), lambda i: (0, i)),
        ],
        out_specs=[pl.BlockSpec((capacity, block), lambda i: (0, i))] * n_experts,
        scratch_shapes=[pltpu.VMEM((n_experts * capacity, tok_count), BF16)],
        compiler_params=params,
        name="dispatch_rows",
    )(route_row, tokens, cotangent)

    swap = flips(halves, 1)
    rows = {0: sent[0]}
    for k in (2, 1, 3):
        rows[k] = lax.ppermute(sent[k], "expert", flips(n_experts, k))
    others = {k: lax.ppermute(rows[k], "tensor", swap) for k in (0, 2, 1, 3)}

    mine, other = {}, {}
    for members in ((2, 0), (3, 1)):
        count = len(members)
        results = pl.pallas_call(
            functools.partial(expert_kernel, n_experts, n_dp, members, capacity),
            out_shape=[shape((capacity, width), BF16)] * (2 * count),
            in_specs=[anywhere] * (n_experts * (n_dp + 1) + 2 * count),
            out_specs=[vmem] * (2 * count),
            scratch_shapes=[
                pltpu.VMEM((n_experts, n_dp, 3 * per, width_part), BF16),
                pltpu.VMEM((count * capacity, width), BF16),
                pltpu.VMEM((count * capacity, width), BF16),
                pltpu.SemaphoreType.DMA((n_experts, n_dp + 1)),
                pltpu.SemaphoreType.DMA((2, count)),
            ],
            compiler_params=params,
            name="expert_math",
        )(
            *[part for parts in weights for part in parts],
            *[rows[k] for k in members],
            *[others[k] for k in members],
        )
        for i, k in enumerate(members):
            kept, given = results[i], results[count + i]
            got = lax.ppermute(given, "tensor", swap)
            total = (kept.astype(F32) + got.astype(F32)).astype(BF16)
            if k:
                total = lax.ppermute(total, "expert", flips(n_experts, k))
            mine[k] = total
            other[k] = lax.ppermute(total, "tensor", swap)

    return tuple(
        pl.pallas_call(
            functools.partial(merge_kernel, n_experts, capacity),
            grid=(width // block,),
            out_shape=[shape((tok_count, width), BF16)] * 2,
            in_specs=[pl.BlockSpec((1, tok_count), lambda i: (0, 0))]
            + [pl.BlockSpec((capacity, block), lambda i: (0, i))] * (2 * n_experts),
            out_specs=[pl.BlockSpec((tok_count, block), lambda i: (0, i))] * 2,
            scratch_shapes=[pltpu.VMEM((n_experts * capacity, tok_count), BF16)],
            compiler_params=params,
            name="merge_rows",
        )(route_row, *[mine[k] for k in range(n_experts)], *[other[k] for k in range(n_experts)])
    )


def expert_math(x_rows, dy_rows, gate_w, up_w, down_w):
    contract = (((1,), (1,)), ((), ()))
    pre_gate = lax.dot_general(x_rows, gate_w, contract, preferred_element_type=jnp.float32)
    pre_up = lax.dot_general(x_rows, up_w, contract, preferred_element_type=jnp.float32)
    sig_gate = jax.nn.sigmoid(pre_gate)
    hidden = (pre_gate * sig_gate * pre_up).astype(jnp.bfloat16)
    out_part = jnp.dot(hidden, down_w, preferred_element_type=jnp.float32)
    grad_hidden = lax.dot_general(dy_rows, down_w, contract, preferred_element_type=jnp.float32)
    grad_gate = (grad_hidden * pre_up * sig_gate * (1.0 + pre_gate * (1.0 - sig_gate))).astype(
        jnp.bfloat16
    )
    grad_up = (grad_hidden * pre_gate * sig_gate).astype(jnp.bfloat16)
    grad_part = jnp.dot(grad_gate, gate_w, preferred_element_type=jnp.float32)
    grad_part = grad_part + jnp.dot(grad_up, up_w, preferred_element_type=jnp.float32)
    return (out_part, grad_part)


def to_tokens(dispatch_table, returned):
    contract = (((0,), (0,)), ((), ()))
    merged = lax.dot_general(dispatch_table, returned, contract, preferred_element_type=jnp.float32)
    return merged.astype(jnp.bfloat16)


def general_plan(tokens, cotangent, routes, cluster, w_gate, w_up, w_down):
    shards = lax.axis_size(("expert", "tensor"))
    source = lax.axis_index(("expert", "tensor"))
    halves = lax.axis_size("tensor")
    rows_dev = w_gate.shape[0]
    width_part = w_gate.shape[1]
    n_experts = cluster.shape[0]
    half_slots = cluster.shape[1] // halves
    per_shard = half_slots // shards
    picks = cluster.reshape(shards, shards, per_shard)
    my_picks = lax.dynamic_index_in_dim(picks, source, 1, keepdims=False)
    is_live = (my_picks >= 0)[:, :, None]
    row_index = jnp.clip(my_picks - source * rows_dev, 0, rows_dev - 1).reshape(-1)

    def select_rows(weight):
        chosen = jnp.take(weight, row_index, axis=0).reshape(shards, per_shard, width_part)
        return jnp.where(is_live, chosen, jnp.zeros((), jnp.bfloat16))

    sent_gate = select_rows(w_gate)
    sent_up = select_rows(w_up)
    sent_down = select_rows(w_down)
    received = (
        lax.all_to_all(sent_gate, ("expert", "tensor"), split_axis=0, concat_axis=0, tiled=True),
        lax.all_to_all(sent_up, ("expert", "tensor"), split_axis=0, concat_axis=0, tiled=True),
        lax.all_to_all(sent_down, ("expert", "tensor"), split_axis=0, concat_axis=0, tiled=True),
    )
    part_gate = received[0].reshape(half_slots, width_part)
    part_up = received[1].reshape(half_slots, width_part)
    part_down = received[2].reshape(half_slots, width_part)
    gate_w, up_w, down_w = (
        lax.all_gather(part_gate, "dp", axis=1, tiled=True),
        lax.all_gather(part_up, "dp", axis=1, tiled=True),
        lax.all_gather(part_down, "dp", axis=1, tiled=True),
    )
    tok_count = tokens.shape[0]
    width = tokens.shape[1]
    capacity = max(2, 3 * tok_count // (2 * n_experts))
    expert_of = routes[:, 0]
    onehot = (expert_of[:, None] == jnp.arange(n_experts, dtype=jnp.int32)[None, :]).astype(
        jnp.int32
    )
    position = jnp.sum((jnp.cumsum(onehot, axis=0) - 1) * onehot, axis=1)
    slot_id = expert_of * capacity + position
    buffer_rows = n_experts * capacity
    dispatch_table = (slot_id[None, :] == jnp.arange(buffer_rows, dtype=jnp.int32)[:, None]).astype(
        jnp.bfloat16
    )
    sent_tokens = jnp.dot(dispatch_table, tokens, preferred_element_type=jnp.float32).astype(
        jnp.bfloat16
    )
    sent_grads = jnp.dot(dispatch_table, cotangent, preferred_element_type=jnp.float32).astype(
        jnp.bfloat16
    )
    sent_tokens = sent_tokens.reshape(n_experts, capacity, width)
    sent_grads = sent_grads.reshape(n_experts, capacity, width)
    x_rows, dy_rows = (
        lax.all_to_all(sent_tokens, "expert", split_axis=0, concat_axis=0, tiled=True),
        lax.all_to_all(sent_grads, "expert", split_axis=0, concat_axis=0, tiled=True),
    )
    x_rows = x_rows.reshape(buffer_rows, width)
    dy_rows = dy_rows.reshape(buffer_rows, width)
    out_part, grad_part = expert_math(x_rows, dy_rows, gate_w, up_w, down_w)
    out_total, grad_total = (
        lax.psum(out_part.astype(jnp.bfloat16), "tensor").astype(jnp.float32),
        lax.psum(grad_part.astype(jnp.bfloat16), "tensor").astype(jnp.float32),
    )
    out_back = out_total.astype(jnp.bfloat16).reshape(n_experts, capacity, width)
    grad_back = grad_total.astype(jnp.bfloat16).reshape(n_experts, capacity, width)
    out_home, grad_home = (
        lax.all_to_all(out_back, "expert", split_axis=0, concat_axis=0, tiled=True),
        lax.all_to_all(grad_back, "expert", split_axis=0, concat_axis=0, tiled=True),
    )
    layer_out = to_tokens(dispatch_table, out_home.reshape(buffer_rows, width))
    grad_out = to_tokens(dispatch_table, grad_home.reshape(buffer_rows, width))
    return (layer_out, grad_out)


def per_device(tokens, cotangent, routes, cluster, w_gate, w_up, w_down):
    n_experts = lax.axis_size("expert")
    halves = lax.axis_size("tensor")
    per = cluster.shape[1] // (halves * n_experts)
    capacity = 3 * tokens.shape[0] // (2 * n_experts)
    aligned = (
        per // halves % 16 == 0
        and capacity % 16 == 0
        and n_experts == 4
        and halves == 2
        and lax.axis_size("dp") == 4
    )
    plan = aligned_plan if aligned else general_plan
    return plan(tokens, cotangent, routes, cluster, w_gate, w_up, w_down)


def solution(mesh):
    in_specs = (
        P(("dp", "expert"), None),
        P(("dp", "expert"), None),
        P(("dp", "expert"), None),
        P(),
        P(("expert", "tensor"), "dp"),
        P(("expert", "tensor"), "dp"),
        P(("expert", "tensor"), "dp"),
    )
    out_specs = (P(("dp", "expert"), None), P(("dp", "expert"), None))
    return jax.shard_map(
        per_device, mesh=mesh, in_specs=in_specs, out_specs=out_specs, check_vma=False
    )
```

```python
import functools

import jax
import jax.numpy as jnp
from jax import lax
from jax.experimental import pallas as pl
from jax.experimental.pallas import tpu as pltpu
from jax.sharding import PartitionSpec as P

BF16 = jnp.bfloat16
F32 = jnp.float32
LAST = (((1,), (1,)), ((), ()))
FIRST = (((0,), (0,)), ((), ()))
VMEM_LIMIT = 16 * 1024 * 1024
MOST_VMEM = 60 * 1024 * 1024


def flips(size, step):
    return [(i, i ^ step) for i in range(size)]


def select_kernel(n_experts, halves, shards, cluster_hbm, gate_hbm, up_hbm, down_hbm, *refs):
    out_refs, scratch, sems = refs[:n_experts], refs[n_experts:-1], refs[-1]
    sources = (cluster_hbm, gate_hbm, up_hbm, down_hbm)
    copies = [pltpu.make_async_copy(a, b, sems.at[i]) for i, (a, b) in enumerate(zip(sources, scratch))]
    for copy in copies:
        copy.start()
    cluster_ref, *weight_refs = scratch
    copies[0].wait()
    mine = lax.axis_index("expert")
    source = mine * halves + lax.axis_index("tensor")
    slots = cluster_ref.shape[1]
    rows = gate_hbm.shape[0]
    half = slots // halves
    run = half // shards
    wide = n_experts * halves * run
    lane = lax.broadcasted_iota(jnp.int32, (8, slots), 1)
    picks = jnp.full((8, slots), -1, jnp.int32)
    for k in range(n_experts):
        row = cluster_ref[pl.ds(mine ^ k, 1), :]
        row = jnp.broadcast_to(row, (8, slots))
        for q in range(halves):
            start = (k * halves + q) * run
            shift = lax.rem(start + 2 * slots - q * half - source * run, slots)
            moved = pltpu.roll(row, shift, 1)
            picks = jnp.where((lane >= start) & (lane < start + run), moved, picks)
    local = jnp.where(picks >= 0, picks - source * rows, -1)[0:1, :wide]
    neuron = lax.broadcasted_iota(jnp.int32, (rows, wide), 0)
    table = jnp.where(neuron == local, 1.0, 0.0).astype(BF16)
    per = halves * run
    for w, ref in enumerate(weight_refs):
        copies[w + 1].wait()
        chosen = lax.dot_general(table, ref[...], FIRST, preferred_element_type=F32).astype(BF16)
        for k in range(n_experts):
            out_refs[k][w * per:(w + 1) * per, :] = chosen[k * per:(k + 1) * per]


def slot_table(routes, n_experts, capacity):
    tokens = routes.shape[1]
    across = jnp.broadcast_to(routes, (tokens, tokens))
    down = jnp.transpose(across)
    i = lax.broadcasted_iota(jnp.int32, (tokens, tokens), 0)
    j = lax.broadcasted_iota(jnp.int32, (tokens, tokens), 1)
    before = jnp.where((across == down) & (i < j), 1, 0)
    position = jnp.sum(before, axis=0, keepdims=True)
    slot = (routes ^ lax.axis_index("expert")) * capacity + position
    number = lax.broadcasted_iota(jnp.int32, (n_experts * capacity, tokens), 0)
    return jnp.where(number == slot, 1.0, 0.0).astype(BF16)


def dispatch_kernel(n_experts, capacity, routes_ref, tokens_ref, cotangent_ref, *refs):
    out_refs, table_ref = refs[:-1], refs[-1]

    @pl.when(pl.program_id(0) == 0)
    def _():
        table_ref[...] = slot_table(routes_ref[...], n_experts, capacity)

    def send(source_ref):
        sent = jnp.dot(table_ref[...], source_ref[...], preferred_element_type=F32).astype(BF16)
        for k in range(n_experts):
            out_refs[k][...] = sent[k * capacity:(k + 1) * capacity]

    core = lax.axis_index("tensor")
    pl.when(core == 0)(lambda: send(tokens_ref))
    pl.when(core != 0)(lambda: send(cotangent_ref))


def merge_kernel(n_experts, capacity, routes_ref, *refs):
    mine_refs, other_refs = refs[:n_experts], refs[n_experts:2 * n_experts]
    out_ref, grad_ref, table_ref = refs[2 * n_experts:]

    @pl.when(pl.program_id(0) == 0)
    def _():
        table_ref[...] = slot_table(routes_ref[...], n_experts, capacity)

    def home(parts):
        rows = jnp.concatenate([part[...] for part in parts], axis=0)
        return lax.dot_general(table_ref[...], rows, FIRST, preferred_element_type=F32).astype(BF16)

    def both(first, second):
        out_ref[...] = home(first)
        grad_ref[...] = home(second)

    core = lax.axis_index("tensor")
    pl.when(core == 0)(lambda: both(mine_refs, other_refs))
    pl.when(core != 0)(lambda: both(other_refs, mine_refs))


def expert_kernel(n_experts, n_dp, n_rows, *refs):
    refs = list(refs)
    weights = [[refs.pop(0) for _ in range(n_dp + 1)] for _ in range(n_experts)]
    mine_refs = [refs.pop(0) for _ in range(n_rows)]
    other_refs = [refs.pop(0) for _ in range(n_rows)]
    keep_refs = [refs.pop(0) for _ in range(n_rows)]
    give_refs = [refs.pop(0) for _ in range(n_rows)]
    me = lax.axis_index("dp")
    first = lax.axis_index("tensor") == 0
    deep, width = weights[0][0].shape
    capacity = mine_refs[0].shape[0]
    per, cut = deep // 3, deep // 2

    def columns(j):
        return pl.ds(pl.multiple_of((me ^ j) * width, width), width)

    def kind(j, w):
        parts = []
        lower, upper = w * per, (w + 1) * per
        for k in range(n_experts):
            if j < n_dp - 1:
                parts.append(weights[k][j][lower:upper, :])
                continue
            if lower < cut:
                parts.append(weights[k][j][lower:min(upper, cut), :])
            if upper > cut:
                parts.append(weights[k][j + 1][max(lower, cut) - cut:upper - cut, :])
        return jnp.concatenate(parts, axis=0)

    pre_gate = pre_up = grad_hidden = 0.0
    for j in range(n_dp):
        mine = jnp.concatenate([ref[:, columns(j)] for ref in mine_refs], axis=0)
        other = jnp.concatenate([ref[:, columns(j)] for ref in other_refs], axis=0)
        x = jnp.where(first, mine, other)
        dy = jnp.where(first, other, mine)
        pre_gate += lax.dot_general(x, kind(j, 0), LAST, preferred_element_type=F32)
        pre_up += lax.dot_general(x, kind(j, 1), LAST, preferred_element_type=F32)
        grad_hidden += lax.dot_general(dy, kind(j, 2), LAST, preferred_element_type=F32)
    sig = jax.nn.sigmoid(pre_gate)
    hidden = (pre_gate * sig * pre_up).astype(BF16)
    grad_gate = (grad_hidden * pre_up * sig * (1.0 + pre_gate * (1.0 - sig))).astype(BF16)
    grad_up = (grad_hidden * pre_gate * sig).astype(BF16)
    for j in range(n_dp):
        out = jnp.dot(hidden, kind(j, 2), preferred_element_type=F32)
        grad = jnp.dot(grad_gate, kind(j, 0), preferred_element_type=F32)
        grad = grad + jnp.dot(grad_up, kind(j, 1), preferred_element_type=F32)
        kept = jnp.where(first, out, grad).astype(BF16)
        given = jnp.where(first, grad, out).astype(BF16)
        for i in range(n_rows):
            at = slice(i * capacity, (i + 1) * capacity)
            keep_refs[i][:, columns(j)] = kept[at]
            give_refs[i][:, columns(j)] = given[at]


def after(values, awaited):
    return lax.optimization_barrier((tuple(values), tuple(awaited)))[0]


def aligned_plan(tokens, cotangent, routes, cluster, w_gate, w_up, w_down):
    n_dp = lax.axis_size("dp")
    n_experts = lax.axis_size("expert")
    halves = lax.axis_size("tensor")
    shards = n_experts * halves
    width_part = w_gate.shape[1]
    tok_count, width = tokens.shape
    run = cluster.shape[1] // (halves * shards)
    per = halves * run
    capacity = 3 * tok_count // (2 * n_experts)
    params = pltpu.CompilerParams(vmem_limit_bytes=VMEM_LIMIT)
    vmem = pl.BlockSpec(memory_space=pltpu.VMEM)
    shape = jax.ShapeDtypeStruct

    sent_w = pl.pallas_call(
        functools.partial(select_kernel, n_experts, halves, shards),
        out_shape=[shape((3 * per, width_part), BF16)] * n_experts,
        in_specs=[pl.BlockSpec(memory_space=pltpu.HBM)] * 4,
        out_specs=[vmem] * n_experts,
        scratch_shapes=[pltpu.VMEM(cluster.shape, jnp.int32)]
        + [pltpu.VMEM(w_gate.shape, BF16)] * 3
        + [pltpu.SemaphoreType.DMA((4,))],
        compiler_params=pltpu.CompilerParams(vmem_limit_bytes=MOST_VMEM),
        name="select_rows",
    )(cluster, w_gate, w_up, w_down)

    def planes(chunk, k):
        return lax.ppermute(chunk, "expert", flips(n_experts, k))

    weights = [None] * n_experts
    arrived = {}
    near_far = {}

    def over_dp(k, awaited):
        (chunk,) = after([arrived[k]], [awaited])
        near_far[k] = (
            lax.ppermute(chunk, "dp", flips(n_dp, 1)),
            lax.ppermute(chunk, "dp", flips(n_dp, 2)),
        )

    def over_dp_far(k):
        near, far = near_far[k]
        cut = near.shape[0] // 2
        low = lax.ppermute(near[:cut], "dp", flips(n_dp, 2))
        high = lax.ppermute(far[cut:], "dp", flips(n_dp, 1))
        weights[k] = [arrived[k], near, far, low, high]

    arrived[0] = sent_w[0]
    arrived[3] = planes(sent_w[3], 3)
    arrived[1] = planes(sent_w[1], 1)
    over_dp(0, [])
    over_dp_far(0)
    arrived[2] = planes(after([sent_w[2]], [arrived[1]])[0], 2)
    over_dp(1, near_far[0])
    over_dp_far(1)
    over_dp(3, (near_far[1], weights[0][3:]))
    over_dp_far(3)
    over_dp(2, (near_far[3], weights[1][3:]))
    over_dp_far(2)

    route_row = routes.reshape(1, tok_count)
    block = width // 4
    sent = pl.pallas_call(
        functools.partial(dispatch_kernel, n_experts, capacity),
        grid=(width // block,),
        out_shape=[shape((capacity, width), BF16)] * n_experts,
        in_specs=[
            pl.BlockSpec((1, tok_count), lambda i: (0, 0)),
            pl.BlockSpec((tok_count, block), lambda i: (0, i)),
            pl.BlockSpec((tok_count, block), lambda i: (0, i)),
        ],
        out_specs=[pl.BlockSpec((capacity, block), lambda i: (0, i))] * n_experts,
        scratch_shapes=[pltpu.VMEM((n_experts * capacity, tok_count), BF16)],
        compiler_params=params,
        name="dispatch_rows",
    )(route_row, tokens, cotangent)

    swap = flips(halves, 1)
    rows = {0: sent[0]}
    early = after([sent[2], sent[1]], [arrived[3], arrived[1]])
    rows[2] = planes(early[0], 2)
    rows[1] = planes(early[1], 1)
    (late,) = after([sent[3]], [arrived[2]])
    rows[3] = planes(late, 3)
    others = {k: lax.ppermute(rows[k], "tensor", swap) for k in (0, 2, 1, 3)}

    mine, other = {}, {}
    returned = []
    for members in ((2, 1), (3, 0)):
        count = len(members)
        here = {k: rows[k] for k in members}
        if returned:
            here[members[0]] = after([rows[members[0]]], returned)[0]
        results = pl.pallas_call(
            functools.partial(expert_kernel, n_experts, n_dp, count),
            out_shape=[shape((capacity, width), BF16)] * (2 * count),
            in_specs=[vmem] * (n_experts * (n_dp + 1) + 2 * count),
            out_specs=[vmem] * (2 * count),
            compiler_params=params,
            cost_estimate=pl.CostEstimate(flops=1000, bytes_accessed=1000, transcendentals=0),
            name="expert_math",
        )(
            *[part for parts in weights for part in parts],
            *[here[k] for k in members],
            *[others[k] for k in members],
        )
        for i, k in enumerate(members):
            kept, given = results[i], results[count + i]
            got = lax.ppermute(given, "tensor", swap)
            total = (kept.astype(F32) + got.astype(F32)).astype(BF16)
            returned.append(total)
            if k == 3:
                (total,) = after([total], [mine[2]])
            if k:
                total = planes(total, k)
            mine[k] = total
            other[k] = lax.ppermute(total, "tensor", swap)

    return tuple(
        pl.pallas_call(
            functools.partial(merge_kernel, n_experts, capacity),
            grid=(width // block,),
            out_shape=[shape((tok_count, width), BF16)] * 2,
            in_specs=[pl.BlockSpec((1, tok_count), lambda i: (0, 0))]
            + [pl.BlockSpec((capacity, block), lambda i: (0, i))] * (2 * n_experts),
            out_specs=[pl.BlockSpec((tok_count, block), lambda i: (0, i))] * 2,
            scratch_shapes=[pltpu.VMEM((n_experts * capacity, tok_count), BF16)],
            compiler_params=params,
            name="merge_rows",
        )(route_row, *[mine[k] for k in range(n_experts)], *[other[k] for k in range(n_experts)])
    )


def expert_math(x_rows, dy_rows, gate_w, up_w, down_w):
    contract = (((1,), (1,)), ((), ()))
    pre_gate = lax.dot_general(x_rows, gate_w, contract, preferred_element_type=jnp.float32)
    pre_up = lax.dot_general(x_rows, up_w, contract, preferred_element_type=jnp.float32)
    sig_gate = jax.nn.sigmoid(pre_gate)
    hidden = (pre_gate * sig_gate * pre_up).astype(jnp.bfloat16)
    out_part = jnp.dot(hidden, down_w, preferred_element_type=jnp.float32)
    grad_hidden = lax.dot_general(dy_rows, down_w, contract, preferred_element_type=jnp.float32)
    grad_gate = (grad_hidden * pre_up * sig_gate * (1.0 + pre_gate * (1.0 - sig_gate))).astype(
        jnp.bfloat16
    )
    grad_up = (grad_hidden * pre_gate * sig_gate).astype(jnp.bfloat16)
    grad_part = jnp.dot(grad_gate, gate_w, preferred_element_type=jnp.float32)
    grad_part = grad_part + jnp.dot(grad_up, up_w, preferred_element_type=jnp.float32)
    return (out_part, grad_part)


def to_tokens(dispatch_table, returned):
    contract = (((0,), (0,)), ((), ()))
    merged = lax.dot_general(dispatch_table, returned, contract, preferred_element_type=jnp.float32)
    return merged.astype(jnp.bfloat16)


def general_plan(tokens, cotangent, routes, cluster, w_gate, w_up, w_down):
    shards = lax.axis_size(("expert", "tensor"))
    source = lax.axis_index(("expert", "tensor"))
    halves = lax.axis_size("tensor")
    rows_dev = w_gate.shape[0]
    width_part = w_gate.shape[1]
    n_experts = cluster.shape[0]
    half_slots = cluster.shape[1] // halves
    per_shard = half_slots // shards
    picks = cluster.reshape(shards, shards, per_shard)
    my_picks = lax.dynamic_index_in_dim(picks, source, 1, keepdims=False)
    is_live = (my_picks >= 0)[:, :, None]
    row_index = jnp.clip(my_picks - source * rows_dev, 0, rows_dev - 1).reshape(-1)

    def select_rows(weight):
        chosen = jnp.take(weight, row_index, axis=0).reshape(shards, per_shard, width_part)
        return jnp.where(is_live, chosen, jnp.zeros((), jnp.bfloat16))

    sent_gate = select_rows(w_gate)
    sent_up = select_rows(w_up)
    sent_down = select_rows(w_down)
    received = (
        lax.all_to_all(sent_gate, ("expert", "tensor"), split_axis=0, concat_axis=0, tiled=True),
        lax.all_to_all(sent_up, ("expert", "tensor"), split_axis=0, concat_axis=0, tiled=True),
        lax.all_to_all(sent_down, ("expert", "tensor"), split_axis=0, concat_axis=0, tiled=True),
    )
    part_gate = received[0].reshape(half_slots, width_part)
    part_up = received[1].reshape(half_slots, width_part)
    part_down = received[2].reshape(half_slots, width_part)
    gate_w, up_w, down_w = (
        lax.all_gather(part_gate, "dp", axis=1, tiled=True),
        lax.all_gather(part_up, "dp", axis=1, tiled=True),
        lax.all_gather(part_down, "dp", axis=1, tiled=True),
    )
    tok_count = tokens.shape[0]
    width = tokens.shape[1]
    capacity = max(2, 3 * tok_count // (2 * n_experts))
    expert_of = routes[:, 0]
    onehot = (expert_of[:, None] == jnp.arange(n_experts, dtype=jnp.int32)[None, :]).astype(
        jnp.int32
    )
    position = jnp.sum((jnp.cumsum(onehot, axis=0) - 1) * onehot, axis=1)
    slot_id = expert_of * capacity + position
    buffer_rows = n_experts * capacity
    dispatch_table = (slot_id[None, :] == jnp.arange(buffer_rows, dtype=jnp.int32)[:, None]).astype(
        jnp.bfloat16
    )
    sent_tokens = jnp.dot(dispatch_table, tokens, preferred_element_type=jnp.float32).astype(
        jnp.bfloat16
    )
    sent_grads = jnp.dot(dispatch_table, cotangent, preferred_element_type=jnp.float32).astype(
        jnp.bfloat16
    )
    sent_tokens = sent_tokens.reshape(n_experts, capacity, width)
    sent_grads = sent_grads.reshape(n_experts, capacity, width)
    x_rows, dy_rows = (
        lax.all_to_all(sent_tokens, "expert", split_axis=0, concat_axis=0, tiled=True),
        lax.all_to_all(sent_grads, "expert", split_axis=0, concat_axis=0, tiled=True),
    )
    x_rows = x_rows.reshape(buffer_rows, width)
    dy_rows = dy_rows.reshape(buffer_rows, width)
    out_part, grad_part = expert_math(x_rows, dy_rows, gate_w, up_w, down_w)
    out_total, grad_total = (
        lax.psum(out_part.astype(jnp.bfloat16), "tensor").astype(jnp.float32),
        lax.psum(grad_part.astype(jnp.bfloat16), "tensor").astype(jnp.float32),
    )
    out_back = out_total.astype(jnp.bfloat16).reshape(n_experts, capacity, width)
    grad_back = grad_total.astype(jnp.bfloat16).reshape(n_experts, capacity, width)
    out_home, grad_home = (
        lax.all_to_all(out_back, "expert", split_axis=0, concat_axis=0, tiled=True),
        lax.all_to_all(grad_back, "expert", split_axis=0, concat_axis=0, tiled=True),
    )
    layer_out = to_tokens(dispatch_table, out_home.reshape(buffer_rows, width))
    grad_out = to_tokens(dispatch_table, grad_home.reshape(buffer_rows, width))
    return (layer_out, grad_out)


def per_device(tokens, cotangent, routes, cluster, w_gate, w_up, w_down):
    n_experts = lax.axis_size("expert")
    halves = lax.axis_size("tensor")
    per = cluster.shape[1] // (halves * n_experts)
    capacity = 3 * tokens.shape[0] // (2 * n_experts)
    aligned = (
        per // halves % 16 == 0
        and capacity % 16 == 0
        and n_experts == 4
        and halves == 2
        and lax.axis_size("dp") == 4
    )
    plan = aligned_plan if aligned else general_plan
    return plan(tokens, cotangent, routes, cluster, w_gate, w_up, w_down)


def solution(mesh):
    in_specs = (
        P(("dp", "expert"), None),
        P(("dp", "expert"), None),
        P(("dp", "expert"), None),
        P(),
        P(("expert", "tensor"), "dp"),
        P(("expert", "tensor"), "dp"),
        P(("expert", "tensor"), "dp"),
    )
    out_specs = (P(("dp", "expert"), None), P(("dp", "expert"), None))
    return jax.shard_map(
        per_device, mesh=mesh, in_specs=in_specs, out_specs=out_specs, check_vma=False
    )
```

```python
import functools

import jax
import jax.numpy as jnp
from jax import lax
from jax.experimental import pallas as pl
from jax.experimental.pallas import tpu as pltpu
from jax.sharding import PartitionSpec as P

BF16 = jnp.bfloat16
F32 = jnp.float32
LAST = (((1,), (1,)), ((), ()))
FIRST = (((0,), (0,)), ((), ()))
VMEM_LIMIT = 16 * 1024 * 1024
MOST_VMEM = 60 * 1024 * 1024


def flips(size, step):
    return [(i, i ^ step) for i in range(size)]


def select_kernel(n_experts, halves, shards, cluster_hbm, gate_hbm, up_hbm, down_hbm, *refs):
    out_refs, scratch = refs[:n_experts], refs[n_experts:-3]
    chosen_ref, sems, out_sems = refs[-3:]
    sources = (cluster_hbm, gate_hbm, up_hbm, down_hbm)
    copies = [pltpu.make_async_copy(a, b, sems.at[i]) for i, (a, b) in enumerate(zip(sources, scratch))]
    for copy in copies:
        copy.start()
    cluster_ref, *weight_refs = scratch
    copies[0].wait()
    mine = lax.axis_index("expert")
    source = mine * halves + lax.axis_index("tensor")
    slots = cluster_ref.shape[1]
    rows = gate_hbm.shape[0]
    half = slots // halves
    run = half // shards
    wide = n_experts * halves * run
    lane = lax.broadcasted_iota(jnp.int32, (8, slots), 1)
    picks = jnp.full((8, slots), -1, jnp.int32)
    for k in range(n_experts):
        row = cluster_ref[pl.ds(mine ^ k, 1), :]
        row = jnp.broadcast_to(row, (8, slots))
        for q in range(halves):
            start = (k * halves + q) * run
            shift = lax.rem(start + 2 * slots - q * half - source * run, slots)
            moved = pltpu.roll(row, shift, 1)
            picks = jnp.where((lane >= start) & (lane < start + run), moved, picks)
    local = jnp.where(picks >= 0, picks - source * rows, -1)[0:1, :wide]
    neuron = lax.broadcasted_iota(jnp.int32, (rows, wide), 0)
    table = jnp.where(neuron == local, 1.0, 0.0).astype(BF16)
    per = halves * run
    sent = []
    for w, ref in enumerate(weight_refs):
        copies[w + 1].wait()
        chosen_ref[w] = lax.dot_general(table, ref[...], FIRST, preferred_element_type=F32).astype(BF16)
        for k in range(n_experts):
            part, place = chosen_ref.at[w, pl.ds(k * per, per)], out_refs[k].at[pl.ds(w * per, per)]
            sent.append(pltpu.make_async_copy(part, place, out_sems.at[w, k]))
            sent[-1].start()
    for copy in sent:
        copy.wait()


def slot_table(routes, n_experts, capacity):
    tokens = routes.shape[1]
    across = jnp.broadcast_to(routes, (tokens, tokens))
    down = jnp.transpose(across)
    i = lax.broadcasted_iota(jnp.int32, (tokens, tokens), 0)
    j = lax.broadcasted_iota(jnp.int32, (tokens, tokens), 1)
    before = jnp.where((across == down) & (i < j), 1, 0)
    position = jnp.sum(before, axis=0, keepdims=True)
    slot = (routes ^ lax.axis_index("expert")) * capacity + position
    number = lax.broadcasted_iota(jnp.int32, (n_experts * capacity, tokens), 0)
    return jnp.where(number == slot, 1.0, 0.0).astype(BF16)


def dispatch_kernel(n_experts, capacity, routes_ref, tokens_ref, cotangent_ref, *refs):
    out_refs, table_ref = refs[:-1], refs[-1]

    @pl.when(pl.program_id(0) == 0)
    def _():
        table_ref[...] = slot_table(routes_ref[...], n_experts, capacity)

    def send(source_ref):
        sent = jnp.dot(table_ref[...], source_ref[...], preferred_element_type=F32).astype(BF16)
        for k in range(n_experts):
            out_refs[k][...] = sent[k * capacity:(k + 1) * capacity]

    core = lax.axis_index("tensor")
    pl.when(core == 0)(lambda: send(tokens_ref))
    pl.when(core != 0)(lambda: send(cotangent_ref))


def merge_kernel(order, capacity, blocks, *refs):
    n_experts = len(order)
    mine_refs, other_refs = refs[:n_experts], refs[n_experts:2 * n_experts]
    routes_ref, out_ref, grad_ref, held_ref, sems = refs[2 * n_experts:]
    table = slot_table(routes_ref[...], n_experts, capacity)
    width = out_ref.shape[1] // blocks
    first = lax.axis_index("tensor") == 0
    copies = []
    for i in range(blocks):
        at = pl.ds(i * width, width)

        def rows(refs):
            return jnp.concatenate([refs[order.index(k)][:, at] for k in range(n_experts)], axis=0)

        mine, other = rows(mine_refs), rows(other_refs)
        for w, (a, b, ref) in enumerate(((mine, other, out_ref), (other, mine, grad_ref))):
            total = lax.dot_general(table, jnp.where(first, a, b), FIRST, preferred_element_type=F32)
            held_ref[w, :, at] = total.astype(BF16)
            copies.append(pltpu.make_async_copy(held_ref.at[w, :, at], ref.at[:, at], sems.at[w, i]))
            copies[-1].start()
    for copy in copies:
        copy.wait()


def expert_kernel(n_parts, n_dp, n_rows, *refs):
    refs = list(refs)
    n_experts = len(n_parts)
    weights = [[refs.pop(0) for _ in range(count)] for count in n_parts]
    mine_refs = [refs.pop(0) for _ in range(n_rows)]
    other_refs = [refs.pop(0) for _ in range(n_rows)]
    keep_refs = [refs.pop(0) for _ in range(n_rows)]
    give_refs = [refs.pop(0) for _ in range(n_rows)]
    me = lax.axis_index("dp")
    first = lax.axis_index("tensor") == 0
    deep, width = weights[0][0].shape
    capacity = mine_refs[0].shape[0]
    per, cut = deep // 3, deep // 2

    def columns(j):
        return pl.ds(pl.multiple_of((me ^ j) * width, width), width)

    def kind(j, w):
        parts = []
        lower, upper = w * per, (w + 1) * per
        for k in range(n_experts):
            if j < n_dp - 1 or n_parts[k] == n_dp:
                parts.append(weights[k][j][lower:upper, :])
                continue
            if lower < cut:
                parts.append(weights[k][j][lower:min(upper, cut), :])
            if upper > cut:
                parts.append(weights[k][j + 1][max(lower, cut) - cut:upper - cut, :])
        return jnp.concatenate(parts, axis=0)

    pre_gate = pre_up = grad_hidden = 0.0
    for j in range(n_dp):
        mine = jnp.concatenate([ref[:, columns(j)] for ref in mine_refs], axis=0)
        other = jnp.concatenate([ref[:, columns(j)] for ref in other_refs], axis=0)
        x = jnp.where(first, mine, other)
        dy = jnp.where(first, other, mine)
        pre_gate += lax.dot_general(x, kind(j, 0), LAST, preferred_element_type=F32)
        pre_up += lax.dot_general(x, kind(j, 1), LAST, preferred_element_type=F32)
        grad_hidden += lax.dot_general(dy, kind(j, 2), LAST, preferred_element_type=F32)
    sig = jax.nn.sigmoid(pre_gate)
    hidden = (pre_gate * sig * pre_up).astype(BF16)
    grad_gate = (grad_hidden * pre_up * sig * (1.0 + pre_gate * (1.0 - sig))).astype(BF16)
    grad_up = (grad_hidden * pre_gate * sig).astype(BF16)
    for j in range(n_dp):
        out = jnp.dot(hidden, kind(j, 2), preferred_element_type=F32)
        grad = jnp.dot(grad_gate, kind(j, 0), preferred_element_type=F32)
        grad = grad + jnp.dot(grad_up, kind(j, 1), preferred_element_type=F32)
        kept = jnp.where(first, out, grad).astype(BF16)
        given = jnp.where(first, grad, out).astype(BF16)
        for i in range(n_rows):
            at = slice(i * capacity, (i + 1) * capacity)
            keep_refs[i][:, columns(j)] = kept[at]
            give_refs[i][:, columns(j)] = given[at]


def after(values, awaited):
    return lax.optimization_barrier((tuple(values), tuple(awaited)))[0]


def aligned_plan(tokens, cotangent, routes, cluster, w_gate, w_up, w_down):
    n_dp = lax.axis_size("dp")
    n_experts = lax.axis_size("expert")
    halves = lax.axis_size("tensor")
    shards = n_experts * halves
    width_part = w_gate.shape[1]
    tok_count, width = tokens.shape
    run = cluster.shape[1] // (halves * shards)
    per = halves * run
    capacity = 3 * tok_count // (2 * n_experts)
    params = pltpu.CompilerParams(vmem_limit_bytes=VMEM_LIMIT)
    vmem = pl.BlockSpec(memory_space=pltpu.VMEM)
    shape = jax.ShapeDtypeStruct

    sent_w = pl.pallas_call(
        functools.partial(select_kernel, n_experts, halves, shards),
        out_shape=[shape((3 * per, width_part), BF16)] * n_experts,
        in_specs=[pl.BlockSpec(memory_space=pltpu.HBM)] * 4,
        out_specs=[pl.BlockSpec(memory_space=pltpu.HBM)] * n_experts,
        scratch_shapes=[pltpu.VMEM(cluster.shape, jnp.int32)]
        + [pltpu.VMEM(w_gate.shape, BF16)] * 3
        + [
            pltpu.VMEM((3, n_experts * per, width_part), BF16),
            pltpu.SemaphoreType.DMA((4,)),
            pltpu.SemaphoreType.DMA((3, n_experts)),
        ],
        compiler_params=pltpu.CompilerParams(vmem_limit_bytes=MOST_VMEM),
        name="select_rows",
    )(cluster, w_gate, w_up, w_down)

    route_row = routes.reshape(1, tok_count)
    block = width // 4
    sent = pl.pallas_call(
        functools.partial(dispatch_kernel, n_experts, capacity),
        grid=(width // block,),
        out_shape=[shape((capacity, width), BF16)] * n_experts,
        in_specs=[
            pl.BlockSpec((1, tok_count), lambda i: (0, 0)),
            pl.BlockSpec((tok_count, block), lambda i: (0, i)),
            pl.BlockSpec((tok_count, block), lambda i: (0, i)),
        ],
        out_specs=[pl.BlockSpec((capacity, block), lambda i: (0, i))] * n_experts,
        scratch_shapes=[pltpu.VMEM((n_experts * capacity, tok_count), BF16)],
        compiler_params=params,
        name="dispatch_rows",
    )(route_row, tokens, cotangent)

    swap = flips(halves, 1)

    def planes(chunk, k):
        return lax.ppermute(chunk, "expert", flips(n_experts, k))

    def spread(chunk, step):
        return lax.ppermute(chunk, "dp", flips(n_dp, step))

    def swapped(chunk):
        return lax.ppermute(chunk, "tensor", swap)

    def direct(chunk):
        return [chunk, spread(chunk, 1), spread(chunk, 2), spread(chunk, 3)]

    def near_far(chunk):
        return [chunk, spread(chunk, 1), spread(chunk, 2)]

    def diagonal(pieces):
        cut = pieces[0].shape[0] // 2
        return [spread(pieces[1][:cut], 2), spread(pieces[2][cut:], 1)]

    weights = [None] * n_experts
    rows, others = {0: sent[0]}, {}
    chunk3 = planes(sent_w[3], 3)
    chunk1 = planes(sent_w[1], 1)
    (sent_w2,) = after([sent_w[2]], [chunk3])
    chunk2 = planes(sent_w2, 2)
    weights[0] = direct(sent_w[0])
    (chunk3,) = after([chunk3], weights[0][1:3])
    pieces3 = near_far(chunk3)
    (chunk1,) = after([chunk1], weights[0][1:])
    pieces1 = near_far(chunk1)
    others[0] = swapped(rows[0])
    (sent_2, sent_1) = after([sent[2], sent[1]], [chunk2, others[0]])
    rows[2] = planes(sent_2, 2)
    rows[1] = planes(sent_1, 1)
    (chunk2,) = after([chunk2], pieces3[1:] + pieces1[1:])
    pieces2 = near_far(chunk2)
    weights[3] = pieces3 + [spread(pieces3[2], 1)]
    weights[1] = pieces1 + [spread(pieces1[1], 2)]
    held2 = after(pieces2[1:], [weights[1][3], weights[3][3]])
    weights[2] = pieces2 + diagonal([chunk2, *held2])
    (sent_3,) = after([sent[3]], [rows[2]])
    rows[3] = planes(sent_3, 3)
    for k in (2, 1, 3):
        others[k] = swapped(rows[k])

    chunk_order = (2, 3, 1, 0)
    mine, other = {}, {}
    returned = []
    for members in ((2, 1), (3, 0)):
        count = len(members)
        here = {k: rows[k] for k in members}
        if returned:
            (here[3],) = after([rows[3]], returned)
        results = pl.pallas_call(
            functools.partial(expert_kernel, [len(weights[k]) for k in chunk_order], n_dp, count),
            out_shape=[shape((capacity, width), BF16)] * (2 * count),
            in_specs=[vmem] * (sum(len(parts) for parts in weights) + 2 * count),
            out_specs=[vmem] * (2 * count),
            compiler_params=params,
            name="expert_math",
        )(
            *[part for k in chunk_order for part in weights[k]],
            *[here[k] for k in members],
            *[others[k] for k in members],
        )
        for i, k in enumerate(members):
            kept, given = results[i], results[count + i]
            got = swapped(given)
            total = (kept.astype(F32) + got.astype(F32)).astype(BF16)
            returned.append(total)
            mine[k] = planes(total, k) if k else total
    other[0] = swapped(mine[0])
    other[2] = swapped(mine[2])
    other[1] = swapped(after([mine[1]], [other[2]])[0])
    other[3] = swapped(after([mine[3]], [other[1]])[0])

    home_order = (2, 1, 0, 3)
    blocks = 8
    return tuple(
        pl.pallas_call(
            functools.partial(merge_kernel, home_order, capacity, blocks),
            out_shape=[shape((tok_count, width), BF16)] * 2,
            in_specs=[vmem] * (2 * n_experts + 1),
            out_specs=[pl.BlockSpec(memory_space=pltpu.HBM)] * 2,
            scratch_shapes=[
                pltpu.VMEM((2, tok_count, width), BF16),
                pltpu.SemaphoreType.DMA((2, blocks)),
            ],
            compiler_params=params,
            name="merge_rows",
        )(*[mine[k] for k in home_order], *[other[k] for k in home_order], route_row)
    )


def expert_math(x_rows, dy_rows, gate_w, up_w, down_w):
    contract = (((1,), (1,)), ((), ()))
    pre_gate = lax.dot_general(x_rows, gate_w, contract, preferred_element_type=jnp.float32)
    pre_up = lax.dot_general(x_rows, up_w, contract, preferred_element_type=jnp.float32)
    sig_gate = jax.nn.sigmoid(pre_gate)
    hidden = (pre_gate * sig_gate * pre_up).astype(jnp.bfloat16)
    out_part = jnp.dot(hidden, down_w, preferred_element_type=jnp.float32)
    grad_hidden = lax.dot_general(dy_rows, down_w, contract, preferred_element_type=jnp.float32)
    grad_gate = (grad_hidden * pre_up * sig_gate * (1.0 + pre_gate * (1.0 - sig_gate))).astype(
        jnp.bfloat16
    )
    grad_up = (grad_hidden * pre_gate * sig_gate).astype(jnp.bfloat16)
    grad_part = jnp.dot(grad_gate, gate_w, preferred_element_type=jnp.float32)
    grad_part = grad_part + jnp.dot(grad_up, up_w, preferred_element_type=jnp.float32)
    return (out_part, grad_part)


def to_tokens(dispatch_table, returned):
    contract = (((0,), (0,)), ((), ()))
    merged = lax.dot_general(dispatch_table, returned, contract, preferred_element_type=jnp.float32)
    return merged.astype(jnp.bfloat16)


def general_plan(tokens, cotangent, routes, cluster, w_gate, w_up, w_down):
    shards = lax.axis_size(("expert", "tensor"))
    source = lax.axis_index(("expert", "tensor"))
    halves = lax.axis_size("tensor")
    rows_dev = w_gate.shape[0]
    width_part = w_gate.shape[1]
    n_experts = cluster.shape[0]
    half_slots = cluster.shape[1] // halves
    per_shard = half_slots // shards
    picks = cluster.reshape(shards, shards, per_shard)
    my_picks = lax.dynamic_index_in_dim(picks, source, 1, keepdims=False)
    is_live = (my_picks >= 0)[:, :, None]
    row_index = jnp.clip(my_picks - source * rows_dev, 0, rows_dev - 1).reshape(-1)

    def select_rows(weight):
        chosen = jnp.take(weight, row_index, axis=0).reshape(shards, per_shard, width_part)
        return jnp.where(is_live, chosen, jnp.zeros((), jnp.bfloat16))

    sent_gate = select_rows(w_gate)
    sent_up = select_rows(w_up)
    sent_down = select_rows(w_down)
    received = (
        lax.all_to_all(sent_gate, ("expert", "tensor"), split_axis=0, concat_axis=0, tiled=True),
        lax.all_to_all(sent_up, ("expert", "tensor"), split_axis=0, concat_axis=0, tiled=True),
        lax.all_to_all(sent_down, ("expert", "tensor"), split_axis=0, concat_axis=0, tiled=True),
    )
    part_gate = received[0].reshape(half_slots, width_part)
    part_up = received[1].reshape(half_slots, width_part)
    part_down = received[2].reshape(half_slots, width_part)
    gate_w, up_w, down_w = (
        lax.all_gather(part_gate, "dp", axis=1, tiled=True),
        lax.all_gather(part_up, "dp", axis=1, tiled=True),
        lax.all_gather(part_down, "dp", axis=1, tiled=True),
    )
    tok_count = tokens.shape[0]
    width = tokens.shape[1]
    capacity = max(2, 3 * tok_count // (2 * n_experts))
    expert_of = routes[:, 0]
    onehot = (expert_of[:, None] == jnp.arange(n_experts, dtype=jnp.int32)[None, :]).astype(
        jnp.int32
    )
    position = jnp.sum((jnp.cumsum(onehot, axis=0) - 1) * onehot, axis=1)
    slot_id = expert_of * capacity + position
    buffer_rows = n_experts * capacity
    dispatch_table = (slot_id[None, :] == jnp.arange(buffer_rows, dtype=jnp.int32)[:, None]).astype(
        jnp.bfloat16
    )
    sent_tokens = jnp.dot(dispatch_table, tokens, preferred_element_type=jnp.float32).astype(
        jnp.bfloat16
    )
    sent_grads = jnp.dot(dispatch_table, cotangent, preferred_element_type=jnp.float32).astype(
        jnp.bfloat16
    )
    sent_tokens = sent_tokens.reshape(n_experts, capacity, width)
    sent_grads = sent_grads.reshape(n_experts, capacity, width)
    x_rows, dy_rows = (
        lax.all_to_all(sent_tokens, "expert", split_axis=0, concat_axis=0, tiled=True),
        lax.all_to_all(sent_grads, "expert", split_axis=0, concat_axis=0, tiled=True),
    )
    x_rows = x_rows.reshape(buffer_rows, width)
    dy_rows = dy_rows.reshape(buffer_rows, width)
    out_part, grad_part = expert_math(x_rows, dy_rows, gate_w, up_w, down_w)
    out_total, grad_total = (
        lax.psum(out_part.astype(jnp.bfloat16), "tensor").astype(jnp.float32),
        lax.psum(grad_part.astype(jnp.bfloat16), "tensor").astype(jnp.float32),
    )
    out_back = out_total.astype(jnp.bfloat16).reshape(n_experts, capacity, width)
    grad_back = grad_total.astype(jnp.bfloat16).reshape(n_experts, capacity, width)
    out_home, grad_home = (
        lax.all_to_all(out_back, "expert", split_axis=0, concat_axis=0, tiled=True),
        lax.all_to_all(grad_back, "expert", split_axis=0, concat_axis=0, tiled=True),
    )
    layer_out = to_tokens(dispatch_table, out_home.reshape(buffer_rows, width))
    grad_out = to_tokens(dispatch_table, grad_home.reshape(buffer_rows, width))
    return (layer_out, grad_out)


def per_device(tokens, cotangent, routes, cluster, w_gate, w_up, w_down):
    n_experts = lax.axis_size("expert")
    halves = lax.axis_size("tensor")
    per = cluster.shape[1] // (halves * n_experts)
    capacity = 3 * tokens.shape[0] // (2 * n_experts)
    aligned = (
        per // halves % 16 == 0
        and capacity % 16 == 0
        and n_experts == 4
        and halves == 2
        and lax.axis_size("dp") == 4
    )
    plan = aligned_plan if aligned else general_plan
    return plan(tokens, cotangent, routes, cluster, w_gate, w_up, w_down)


def solution(mesh):
    in_specs = (
        P(("dp", "expert"), None),
        P(("dp", "expert"), None),
        P(("dp", "expert"), None),
        P(),
        P(("expert", "tensor"), "dp"),
        P(("expert", "tensor"), "dp"),
        P(("expert", "tensor"), "dp"),
    )
    out_specs = (P(("dp", "expert"), None), P(("dp", "expert"), None))
    return jax.shard_map(
        per_device, mesh=mesh, in_specs=in_specs, out_specs=out_specs, check_vma=False
    )
```

```python
import functools

import jax
import jax.numpy as jnp
from jax import lax
from jax.experimental import pallas as pl
from jax.experimental.pallas import tpu as pltpu
from jax.sharding import PartitionSpec as P

BF16 = jnp.bfloat16
F32 = jnp.float32
LAST = (((1,), (1,)), ((), ()))
FIRST = (((0,), (0,)), ((), ()))
VMEM_LIMIT = 16 * 1024 * 1024
MOST_VMEM = 60 * 1024 * 1024


def flips(size, step):
    return [(i, i ^ step) for i in range(size)]


def select_kernel(n_experts, halves, shards, cluster_hbm, gate_hbm, up_hbm, down_hbm, *refs):
    out_refs, scratch = refs[:n_experts], refs[n_experts:-3]
    chosen_ref, sems, out_sems = refs[-3:]
    sources = (cluster_hbm, gate_hbm, up_hbm, down_hbm)
    copies = [pltpu.make_async_copy(a, b, sems.at[i]) for i, (a, b) in enumerate(zip(sources, scratch))]
    for copy in copies:
        copy.start()
    cluster_ref, *weight_refs = scratch
    copies[0].wait()
    mine = lax.axis_index("expert")
    source = mine * halves + lax.axis_index("tensor")
    slots = cluster_ref.shape[1]
    rows = gate_hbm.shape[0]
    half = slots // halves
    run = half // shards
    wide = n_experts * halves * run
    lane = lax.broadcasted_iota(jnp.int32, (8, slots), 1)
    picks = jnp.full((8, slots), -1, jnp.int32)
    for k in range(n_experts):
        row = cluster_ref[pl.ds(mine ^ k, 1), :]
        row = jnp.broadcast_to(row, (8, slots))
        for q in range(halves):
            start = (k * halves + q) * run
            shift = lax.rem(start + 2 * slots - q * half - source * run, slots)
            moved = pltpu.roll(row, shift, 1)
            picks = jnp.where((lane >= start) & (lane < start + run), moved, picks)
    local = jnp.where(picks >= 0, picks - source * rows, -1)[0:1, :wide]
    neuron = lax.broadcasted_iota(jnp.int32, (rows, wide), 0)
    table = jnp.where(neuron == local, 1.0, 0.0).astype(BF16)
    per = halves * run
    sent = []
    for w, ref in enumerate(weight_refs):
        copies[w + 1].wait()
        chosen_ref[w] = lax.dot_general(table, ref[...], FIRST, preferred_element_type=F32).astype(BF16)
        for k in range(n_experts):
            part, place = chosen_ref.at[w, pl.ds(k * per, per)], out_refs[k].at[pl.ds(w * per, per)]
            sent.append(pltpu.make_async_copy(part, place, out_sems.at[w, k]))
            sent[-1].start()
    for copy in sent:
        copy.wait()


def slot_table(routes, n_experts, capacity):
    tokens = routes.shape[1]
    across = jnp.broadcast_to(routes, (tokens, tokens))
    down = jnp.transpose(across)
    i = lax.broadcasted_iota(jnp.int32, (tokens, tokens), 0)
    j = lax.broadcasted_iota(jnp.int32, (tokens, tokens), 1)
    before = jnp.where((across == down) & (i < j), 1, 0)
    position = jnp.sum(before, axis=0, keepdims=True)
    slot = (routes ^ lax.axis_index("expert")) * capacity + position
    number = lax.broadcasted_iota(jnp.int32, (n_experts * capacity, tokens), 0)
    return jnp.where(number == slot, 1.0, 0.0).astype(BF16)


def dispatch_kernel(n_experts, capacity, routes_ref, tokens_ref, cotangent_ref, *refs):
    out_refs, local_ref, table_ref = refs[:n_experts], *refs[n_experts:]

    @pl.when(pl.program_id(0) == 0)
    def _():
        table_ref[...] = slot_table(routes_ref[...], n_experts, capacity)

    def rows(source_ref, count):
        return jnp.dot(table_ref[:count], source_ref[...], preferred_element_type=F32).astype(BF16)

    def send(mine_ref, other_ref):
        sent = rows(mine_ref, n_experts * capacity)
        for k in range(n_experts):
            out_refs[k][...] = sent[k * capacity:(k + 1) * capacity]
        local_ref[...] = rows(other_ref, capacity)

    core = lax.axis_index("tensor")
    pl.when(core == 0)(lambda: send(tokens_ref, cotangent_ref))
    pl.when(core != 0)(lambda: send(cotangent_ref, tokens_ref))


def merge_kernel(order, capacity, blocks, *refs):
    n_experts, count = len(order) + 1, len(order)
    mine_refs, other_refs = refs[:count], refs[count:2 * count]
    kept_ref, got_ref, routes_ref, out_ref, grad_ref, held_ref, sems = refs[2 * count:]
    table = slot_table(routes_ref[...], n_experts, capacity)
    width = out_ref.shape[1] // blocks
    first = lax.axis_index("tensor") == 0
    copies = []
    for i in range(blocks):
        at = pl.ds(i * width, width)

        def half(ref, h):
            return ref[h * capacity:(h + 1) * capacity, at].astype(F32)

        def rows(refs, h):
            parts = [refs[order.index(k)][:, at] for k in range(1, n_experts)]
            stayed = (half(kept_ref, h) + half(got_ref, 1 - h)).astype(BF16)
            return jnp.concatenate([stayed, *parts], axis=0)

        mine, other = rows(mine_refs, 0), rows(other_refs, 1)
        for w, (a, b, ref) in enumerate(((mine, other, out_ref), (other, mine, grad_ref))):
            total = lax.dot_general(table, jnp.where(first, a, b), FIRST, preferred_element_type=F32)
            held_ref[w, :, at] = total.astype(BF16)
            copies.append(pltpu.make_async_copy(held_ref.at[w, :, at], ref.at[:, at], sems.at[w, i]))
            copies[-1].start()
    for copy in copies:
        copy.wait()


def expert_kernel(n_parts, n_dp, n_rows, stacked, *refs):
    refs = list(refs)
    n_experts = len(n_parts)
    weights = [[refs.pop(0) for _ in range(count)] for count in n_parts]
    mine_refs = [refs.pop(0) for _ in range(n_rows)]
    other_refs = [refs.pop(0) for _ in range(n_rows)]
    capacity = mine_refs[0].shape[0]
    out_refs = []
    for i in range(n_rows):
        if i == stacked:
            ref = refs.pop(0)
            out_refs.append((ref.at[pl.ds(0, capacity)], ref.at[pl.ds(capacity, capacity)]))
        else:
            out_refs.append((refs.pop(0), refs.pop(0)))
    me = lax.axis_index("dp")
    first = lax.axis_index("tensor") == 0
    deep, width = weights[0][0].shape
    per, cut = deep // 3, deep // 2

    def columns(j):
        return pl.ds(pl.multiple_of((me ^ j) * width, width), width)

    def kind(j, w):
        parts = []
        lower, upper = w * per, (w + 1) * per
        for k in range(n_experts):
            if j < n_dp - 1 or n_parts[k] == n_dp:
                parts.append(weights[k][j][lower:upper, :])
                continue
            if lower < cut:
                parts.append(weights[k][j][lower:min(upper, cut), :])
            if upper > cut:
                parts.append(weights[k][j + 1][max(lower, cut) - cut:upper - cut, :])
        return jnp.concatenate(parts, axis=0)

    pre_gate = pre_up = grad_hidden = 0.0
    for j in range(n_dp):
        mine = jnp.concatenate([ref[:, columns(j)] for ref in mine_refs], axis=0)
        other = jnp.concatenate([ref[:, columns(j)] for ref in other_refs], axis=0)
        x = jnp.where(first, mine, other)
        dy = jnp.where(first, other, mine)
        pre_gate += lax.dot_general(x, kind(j, 0), LAST, preferred_element_type=F32)
        pre_up += lax.dot_general(x, kind(j, 1), LAST, preferred_element_type=F32)
        grad_hidden += lax.dot_general(dy, kind(j, 2), LAST, preferred_element_type=F32)
    sig = jax.nn.sigmoid(pre_gate)
    hidden = (pre_gate * sig * pre_up).astype(BF16)
    grad_gate = (grad_hidden * pre_up * sig * (1.0 + pre_gate * (1.0 - sig))).astype(BF16)
    grad_up = (grad_hidden * pre_gate * sig).astype(BF16)
    for j in range(n_dp):
        out = jnp.dot(hidden, kind(j, 2), preferred_element_type=F32)
        grad = jnp.dot(grad_gate, kind(j, 0), preferred_element_type=F32)
        grad = grad + jnp.dot(grad_up, kind(j, 1), preferred_element_type=F32)
        kept = jnp.where(first, out, grad).astype(BF16)
        given = jnp.where(first, grad, out).astype(BF16)
        for i in range(n_rows):
            at = slice(i * capacity, (i + 1) * capacity)
            keep_ref, give_ref = out_refs[i]
            keep_ref[:, columns(j)] = kept[at]
            give_ref[:, columns(j)] = given[at]


def after(values, awaited):
    return lax.optimization_barrier((tuple(values), tuple(awaited)))[0]


def aligned_plan(tokens, cotangent, routes, cluster, w_gate, w_up, w_down):
    n_dp = lax.axis_size("dp")
    n_experts = lax.axis_size("expert")
    halves = lax.axis_size("tensor")
    shards = n_experts * halves
    width_part = w_gate.shape[1]
    tok_count, width = tokens.shape
    run = cluster.shape[1] // (halves * shards)
    per = halves * run
    capacity = 3 * tok_count // (2 * n_experts)
    params = pltpu.CompilerParams(vmem_limit_bytes=VMEM_LIMIT)
    vmem = pl.BlockSpec(memory_space=pltpu.VMEM)
    shape = jax.ShapeDtypeStruct

    sent_w = pl.pallas_call(
        functools.partial(select_kernel, n_experts, halves, shards),
        out_shape=[shape((3 * per, width_part), BF16)] * n_experts,
        in_specs=[pl.BlockSpec(memory_space=pltpu.HBM)] * 4,
        out_specs=[pl.BlockSpec(memory_space=pltpu.HBM)] * n_experts,
        scratch_shapes=[pltpu.VMEM(cluster.shape, jnp.int32)]
        + [pltpu.VMEM(w_gate.shape, BF16)] * 3
        + [
            pltpu.VMEM((3, n_experts * per, width_part), BF16),
            pltpu.SemaphoreType.DMA((4,)),
            pltpu.SemaphoreType.DMA((3, n_experts)),
        ],
        compiler_params=pltpu.CompilerParams(vmem_limit_bytes=MOST_VMEM),
        name="select_rows",
    )(cluster, w_gate, w_up, w_down)

    route_row = routes.reshape(1, tok_count)
    block = width // 4
    *sent, local = pl.pallas_call(
        functools.partial(dispatch_kernel, n_experts, capacity),
        grid=(width // block,),
        out_shape=[shape((capacity, width), BF16)] * (n_experts + 1),
        in_specs=[
            pl.BlockSpec((1, tok_count), lambda i: (0, 0)),
            pl.BlockSpec((tok_count, block), lambda i: (0, i)),
            pl.BlockSpec((tok_count, block), lambda i: (0, i)),
        ],
        out_specs=[pl.BlockSpec((capacity, block), lambda i: (0, i))] * (n_experts + 1),
        scratch_shapes=[pltpu.VMEM((n_experts * capacity, tok_count), BF16)],
        compiler_params=params,
        name="dispatch_rows",
    )(route_row, tokens, cotangent)

    swap = flips(halves, 1)

    def planes(chunk, k):
        return lax.ppermute(chunk, "expert", flips(n_experts, k))

    def spread(chunk, step):
        return lax.ppermute(chunk, "dp", flips(n_dp, step))

    def swapped(chunk):
        return lax.ppermute(chunk, "tensor", swap)

    def direct(chunk):
        return [chunk, spread(chunk, 1), spread(chunk, 2), spread(chunk, 3)]

    def near_far(chunk):
        return [chunk, spread(chunk, 1), spread(chunk, 2)]

    def diagonal(pieces):
        cut = pieces[0].shape[0] // 2
        return [spread(pieces[1][:cut], 2), spread(pieces[2][cut:], 1)]

    rows, others = {0: sent[0]}, {0: local}
    chunk3, chunk1 = planes(sent_w[3], 3), planes(sent_w[1], 1)
    pieces0 = direct(sent_w[0])
    (sent_w2,) = after([sent_w[2]], [chunk3])
    chunk2 = planes(sent_w2, 2)
    (chunk1,) = after([chunk1], [*pieces0[1:], local])
    pieces1 = near_far(chunk1)
    (chunk3,) = after([chunk3], pieces0[1:3])
    pieces3 = near_far(chunk3)
    (held,) = after([chunk2], pieces3[1:] + pieces1[1:])
    pieces2 = near_far(held)
    for k, awaited in ((2, chunk2), (1, chunk2), (3, None)):
        (row,) = after([sent[k]], [rows[2] if awaited is None else awaited])
        rows[k] = planes(row, k)
    pieces1.append(spread(pieces1[1], 2))
    pieces3.append(spread(pieces3[2], 1))
    held2 = after(pieces2[1:], [pieces1[3], pieces3[3]])
    pieces2 += diagonal([pieces2[0], *held2])
    for k in (2, 1, 3):
        others[k] = swapped(rows[k])

    weights = (pieces3, pieces0, pieces1, pieces2)
    mine, other, returned = {}, {}, []
    for members in ((2, 1), (3, 0)):
        count = len(members)
        here = {k: rows[k] for k in members}
        if returned:
            (here[3],) = after([rows[3]], returned[:1])
        out_shape = []
        for k in members:
            out_shape += [shape((capacity, width), BF16)] * 2 if k else [shape((2 * capacity, width), BF16)]
        results = pl.pallas_call(
            functools.partial(
                expert_kernel,
                [len(pieces) for pieces in weights],
                n_dp,
                count,
                members.index(0) if 0 in members else None,
            ),
            out_shape=out_shape,
            in_specs=[vmem] * (sum(len(pieces) for pieces in weights) + 2 * count),
            out_specs=[vmem] * len(out_shape),
            compiler_params=params,
            name="expert_math",
        )(
            *[piece for pieces in weights for piece in pieces],
            *[here[k] for k in members],
            *[others[k] for k in members],
        )
        results = list(results)
        for k in members:
            if not k:
                stayed = results.pop(0)
                stayed = (stayed, swapped(stayed))
                continue
            kept, given = results.pop(0), results.pop(0)
            total = (kept.astype(F32) + swapped(given).astype(F32)).astype(BF16)
            returned.append(total)
            mine[k] = planes(total, k)
    awaited = []
    for k in (2, 1, 3):
        other[k] = swapped(after([mine[k]], awaited)[0])
        awaited = [other[k]]

    order = (2, 1, 3)
    blocks = 8
    return tuple(
        pl.pallas_call(
            functools.partial(merge_kernel, order, capacity, blocks),
            out_shape=[shape((tok_count, width), BF16)] * 2,
            in_specs=[vmem] * (2 * n_experts + 1),
            out_specs=[pl.BlockSpec(memory_space=pltpu.HBM)] * 2,
            scratch_shapes=[
                pltpu.VMEM((2, tok_count, width), BF16),
                pltpu.SemaphoreType.DMA((2, blocks)),
            ],
            compiler_params=params,
            name="merge_rows",
        )(*[mine[k] for k in order], *[other[k] for k in order], *stayed, route_row)
    )


def expert_math(x_rows, dy_rows, gate_w, up_w, down_w):
    contract = (((1,), (1,)), ((), ()))
    pre_gate = lax.dot_general(x_rows, gate_w, contract, preferred_element_type=jnp.float32)
    pre_up = lax.dot_general(x_rows, up_w, contract, preferred_element_type=jnp.float32)
    sig_gate = jax.nn.sigmoid(pre_gate)
    hidden = (pre_gate * sig_gate * pre_up).astype(jnp.bfloat16)
    out_part = jnp.dot(hidden, down_w, preferred_element_type=jnp.float32)
    grad_hidden = lax.dot_general(dy_rows, down_w, contract, preferred_element_type=jnp.float32)
    grad_gate = (grad_hidden * pre_up * sig_gate * (1.0 + pre_gate * (1.0 - sig_gate))).astype(
        jnp.bfloat16
    )
    grad_up = (grad_hidden * pre_gate * sig_gate).astype(jnp.bfloat16)
    grad_part = jnp.dot(grad_gate, gate_w, preferred_element_type=jnp.float32)
    grad_part = grad_part + jnp.dot(grad_up, up_w, preferred_element_type=jnp.float32)
    return (out_part, grad_part)


def to_tokens(dispatch_table, returned):
    contract = (((0,), (0,)), ((), ()))
    merged = lax.dot_general(dispatch_table, returned, contract, preferred_element_type=jnp.float32)
    return merged.astype(jnp.bfloat16)


def general_plan(tokens, cotangent, routes, cluster, w_gate, w_up, w_down):
    shards = lax.axis_size(("expert", "tensor"))
    source = lax.axis_index(("expert", "tensor"))
    halves = lax.axis_size("tensor")
    rows_dev = w_gate.shape[0]
    width_part = w_gate.shape[1]
    n_experts = cluster.shape[0]
    half_slots = cluster.shape[1] // halves
    per_shard = half_slots // shards
    picks = cluster.reshape(shards, shards, per_shard)
    my_picks = lax.dynamic_index_in_dim(picks, source, 1, keepdims=False)
    is_live = (my_picks >= 0)[:, :, None]
    row_index = jnp.clip(my_picks - source * rows_dev, 0, rows_dev - 1).reshape(-1)

    def select_rows(weight):
        chosen = jnp.take(weight, row_index, axis=0).reshape(shards, per_shard, width_part)
        return jnp.where(is_live, chosen, jnp.zeros((), jnp.bfloat16))

    sent_gate = select_rows(w_gate)
    sent_up = select_rows(w_up)
    sent_down = select_rows(w_down)
    received = (
        lax.all_to_all(sent_gate, ("expert", "tensor"), split_axis=0, concat_axis=0, tiled=True),
        lax.all_to_all(sent_up, ("expert", "tensor"), split_axis=0, concat_axis=0, tiled=True),
        lax.all_to_all(sent_down, ("expert", "tensor"), split_axis=0, concat_axis=0, tiled=True),
    )
    part_gate = received[0].reshape(half_slots, width_part)
    part_up = received[1].reshape(half_slots, width_part)
    part_down = received[2].reshape(half_slots, width_part)
    gate_w, up_w, down_w = (
        lax.all_gather(part_gate, "dp", axis=1, tiled=True),
        lax.all_gather(part_up, "dp", axis=1, tiled=True),
        lax.all_gather(part_down, "dp", axis=1, tiled=True),
    )
    tok_count = tokens.shape[0]
    width = tokens.shape[1]
    capacity = max(2, 3 * tok_count // (2 * n_experts))
    expert_of = routes[:, 0]
    onehot = (expert_of[:, None] == jnp.arange(n_experts, dtype=jnp.int32)[None, :]).astype(
        jnp.int32
    )
    position = jnp.sum((jnp.cumsum(onehot, axis=0) - 1) * onehot, axis=1)
    slot_id = expert_of * capacity + position
    buffer_rows = n_experts * capacity
    dispatch_table = (slot_id[None, :] == jnp.arange(buffer_rows, dtype=jnp.int32)[:, None]).astype(
        jnp.bfloat16
    )
    sent_tokens = jnp.dot(dispatch_table, tokens, preferred_element_type=jnp.float32).astype(
        jnp.bfloat16
    )
    sent_grads = jnp.dot(dispatch_table, cotangent, preferred_element_type=jnp.float32).astype(
        jnp.bfloat16
    )
    sent_tokens = sent_tokens.reshape(n_experts, capacity, width)
    sent_grads = sent_grads.reshape(n_experts, capacity, width)
    x_rows, dy_rows = (
        lax.all_to_all(sent_tokens, "expert", split_axis=0, concat_axis=0, tiled=True),
        lax.all_to_all(sent_grads, "expert", split_axis=0, concat_axis=0, tiled=True),
    )
    x_rows = x_rows.reshape(buffer_rows, width)
    dy_rows = dy_rows.reshape(buffer_rows, width)
    out_part, grad_part = expert_math(x_rows, dy_rows, gate_w, up_w, down_w)
    out_total, grad_total = (
        lax.psum(out_part.astype(jnp.bfloat16), "tensor").astype(jnp.float32),
        lax.psum(grad_part.astype(jnp.bfloat16), "tensor").astype(jnp.float32),
    )
    out_back = out_total.astype(jnp.bfloat16).reshape(n_experts, capacity, width)
    grad_back = grad_total.astype(jnp.bfloat16).reshape(n_experts, capacity, width)
    out_home, grad_home = (
        lax.all_to_all(out_back, "expert", split_axis=0, concat_axis=0, tiled=True),
        lax.all_to_all(grad_back, "expert", split_axis=0, concat_axis=0, tiled=True),
    )
    layer_out = to_tokens(dispatch_table, out_home.reshape(buffer_rows, width))
    grad_out = to_tokens(dispatch_table, grad_home.reshape(buffer_rows, width))
    return (layer_out, grad_out)


def per_device(tokens, cotangent, routes, cluster, w_gate, w_up, w_down):
    n_experts = lax.axis_size("expert")
    halves = lax.axis_size("tensor")
    per = cluster.shape[1] // (halves * n_experts)
    capacity = 3 * tokens.shape[0] // (2 * n_experts)
    aligned = (
        per // halves % 16 == 0
        and capacity % 16 == 0
        and n_experts == 4
        and halves == 2
        and lax.axis_size("dp") == 4
    )
    plan = aligned_plan if aligned else general_plan
    return plan(tokens, cotangent, routes, cluster, w_gate, w_up, w_down)


def solution(mesh):
    in_specs = (
        P(("dp", "expert"), None),
        P(("dp", "expert"), None),
        P(("dp", "expert"), None),
        P(),
        P(("expert", "tensor"), "dp"),
        P(("expert", "tensor"), "dp"),
        P(("expert", "tensor"), "dp"),
    )
    out_specs = (P(("dp", "expert"), None), P(("dp", "expert"), None))
    return jax.shard_map(
        per_device, mesh=mesh, in_specs=in_specs, out_specs=out_specs, check_vma=False
    )
```

```python
import functools

import jax
import jax.numpy as jnp
from jax import lax
from jax.experimental import pallas as pl
from jax.experimental.pallas import tpu as pltpu
from jax.sharding import PartitionSpec as P

BF16 = jnp.bfloat16
F32 = jnp.float32
LAST = (((1,), (1,)), ((), ()))
VMEM_LIMIT = 16 * 1024 * 1024
MOST_VMEM = 60 * 1024 * 1024


def flips(size, step):
    return [(i, i ^ step) for i in range(size)]


def select_kernel(n_experts, halves, shards, cluster_hbm, gate_hbm, up_hbm, down_hbm, *refs):
    out_refs, scratch = refs[:n_experts], refs[n_experts:-3]
    chosen_ref, sems, out_sems = refs[-3:]
    sources = (cluster_hbm, gate_hbm, up_hbm, down_hbm)
    copies = [pltpu.make_async_copy(a, b, sems.at[i]) for i, (a, b) in enumerate(zip(sources, scratch))]
    for copy in copies:
        copy.start()
    cluster_ref, *weight_refs = scratch
    copies[0].wait()
    mine = lax.axis_index("expert")
    source = mine * halves + lax.axis_index("tensor")
    slots = cluster_ref.shape[1]
    rows = gate_hbm.shape[0]
    half = slots // halves
    run = half // shards
    wide = n_experts * halves * run
    lane = lax.broadcasted_iota(jnp.int32, (8, slots), 1)
    picks = jnp.full((8, slots), -1, jnp.int32)
    for k in range(n_experts):
        row = cluster_ref[pl.ds(mine ^ k, 1), :]
        row = jnp.broadcast_to(row, (8, slots))
        for q in range(halves):
            start = (k * halves + q) * run
            shift = lax.rem(start + 2 * slots - q * half - source * run, slots)
            moved = pltpu.roll(row, shift, 1)
            picks = jnp.where((lane >= start) & (lane < start + run), moved, picks)
    local = jnp.where(picks >= 0, picks - source * rows, -1)[0:1, :wide]
    down = jnp.transpose(jnp.broadcast_to(local, (wide, wide)))[:, :1]
    neuron = lax.broadcasted_iota(jnp.int32, (wide, rows), 1)
    table = jnp.where(neuron == down, 1.0, 0.0).astype(BF16)
    per = halves * run
    sent = []
    for w, ref in enumerate(weight_refs):
        copies[w + 1].wait()
        chosen_ref[w] = jnp.dot(table, ref[...], preferred_element_type=F32).astype(BF16)
        for k in range(n_experts):
            part, place = chosen_ref.at[w, pl.ds(k * per, per)], out_refs[k].at[pl.ds(w * per, per)]
            sent.append(pltpu.make_async_copy(part, place, out_sems.at[w, k]))
            sent[-1].start()
    for copy in sent:
        copy.wait()


def slot_table(routes, n_experts, capacity):
    tokens = routes.shape[1]
    across = jnp.broadcast_to(routes, (tokens, tokens))
    down = jnp.transpose(across)
    i = lax.broadcasted_iota(jnp.int32, (tokens, tokens), 0)
    j = lax.broadcasted_iota(jnp.int32, (tokens, tokens), 1)
    before = jnp.where((across == down) & (i < j), 1, 0)
    position = jnp.sum(before, axis=0, keepdims=True)
    slot = (routes ^ lax.axis_index("expert")) * capacity + position
    number = lax.broadcasted_iota(jnp.int32, (n_experts * capacity, tokens), 0)
    return jnp.where(number == slot, 1.0, 0.0)


def dispatch_kernel(n_experts, capacity, routes_ref, tokens_ref, cotangent_ref, *refs):
    out_refs, local_ref, home_ref, table_ref = refs[:n_experts], *refs[n_experts:]

    @pl.when(pl.program_id(0) == 0)
    def _():
        table = slot_table(routes_ref[...], n_experts, capacity)
        table_ref[...] = table.astype(BF16)
        home_ref[...] = jnp.transpose(table).astype(BF16)

    def rows(source_ref, count):
        return jnp.dot(table_ref[:count], source_ref[...], preferred_element_type=F32).astype(BF16)

    def send(mine_ref, other_ref):
        sent = rows(mine_ref, n_experts * capacity)
        for k in range(n_experts):
            out_refs[k][...] = sent[k * capacity:(k + 1) * capacity]
        local_ref[...] = rows(other_ref, capacity)

    core = lax.axis_index("tensor")
    pl.when(core == 0)(lambda: send(tokens_ref, cotangent_ref))
    pl.when(core != 0)(lambda: send(cotangent_ref, tokens_ref))


def merge_kernel(order, capacity, blocks, *refs):
    n_experts, count = len(order) + 1, len(order)
    mine_refs, other_refs = refs[:count], refs[count:2 * count]
    kept_ref, got_ref, table_ref, out_ref, grad_ref, held_ref, sems = refs[2 * count:]
    table = table_ref[...]
    width = out_ref.shape[1] // blocks
    first = lax.axis_index("tensor") == 0
    copies = []
    for i in range(blocks):
        at = pl.ds(i * width, width)

        def half(ref, h):
            return ref[h * capacity:(h + 1) * capacity, at].astype(F32)

        def rows(refs, h):
            parts = [refs[order.index(k)][:, at] for k in range(1, n_experts)]
            stayed = (half(kept_ref, h) + half(got_ref, 1 - h)).astype(BF16)
            return jnp.concatenate([stayed, *parts], axis=0)

        mine, other = rows(mine_refs, 0), rows(other_refs, 1)
        for w, (a, b, ref) in enumerate(((mine, other, out_ref), (other, mine, grad_ref))):
            total = jnp.dot(table, jnp.where(first, a, b), preferred_element_type=F32)
            held_ref[w, :, at] = total.astype(BF16)
            copies.append(pltpu.make_async_copy(held_ref.at[w, :, at], ref.at[:, at], sems.at[w, i]))
            copies[-1].start()
    for copy in copies:
        copy.wait()


def expert_kernel(n_parts, n_dp, n_rows, stacked, *refs):
    refs = list(refs)
    n_experts = len(n_parts)
    weights = [[refs.pop(0) for _ in range(count)] for count in n_parts]
    mine_refs = [refs.pop(0) for _ in range(n_rows)]
    other_refs = [refs.pop(0) for _ in range(n_rows)]
    capacity = mine_refs[0].shape[0]
    out_refs = []
    for i in range(n_rows):
        if i == stacked:
            ref = refs.pop(0)
            out_refs.append((ref.at[pl.ds(0, capacity)], ref.at[pl.ds(capacity, capacity)]))
        else:
            out_refs.append((refs.pop(0), refs.pop(0)))
    me = lax.axis_index("dp")
    first = lax.axis_index("tensor") == 0
    deep, width = weights[0][0].shape
    per, cut = deep // 3, deep // 2

    def columns(j):
        return pl.ds(pl.multiple_of((me ^ j) * width, width), width)

    def kind(j, w):
        parts = []
        lower, upper = w * per, (w + 1) * per
        for k in range(n_experts):
            if j < n_dp - 1 or n_parts[k] == n_dp:
                parts.append(weights[k][j][lower:upper, :])
                continue
            if lower < cut:
                parts.append(weights[k][j][lower:min(upper, cut), :])
            if upper > cut:
                parts.append(weights[k][j + 1][max(lower, cut) - cut:upper - cut, :])
        return jnp.concatenate(parts, axis=0)

    pre_gate = pre_up = grad_hidden = 0.0
    for j in range(n_dp):
        mine = jnp.concatenate([ref[:, columns(j)] for ref in mine_refs], axis=0)
        other = jnp.concatenate([ref[:, columns(j)] for ref in other_refs], axis=0)
        x = jnp.where(first, mine, other)
        dy = jnp.where(first, other, mine)
        pre_gate += lax.dot_general(x, kind(j, 0), LAST, preferred_element_type=F32)
        pre_up += lax.dot_general(x, kind(j, 1), LAST, preferred_element_type=F32)
        grad_hidden += lax.dot_general(dy, kind(j, 2), LAST, preferred_element_type=F32)
    sig = jax.nn.sigmoid(pre_gate)
    hidden = (pre_gate * sig * pre_up).astype(BF16)
    grad_gate = (grad_hidden * pre_up * sig * (1.0 + pre_gate * (1.0 - sig))).astype(BF16)
    grad_up = (grad_hidden * pre_gate * sig).astype(BF16)
    for j in range(n_dp):
        out = jnp.dot(hidden, kind(j, 2), preferred_element_type=F32)
        grad = jnp.dot(grad_gate, kind(j, 0), preferred_element_type=F32)
        grad = grad + jnp.dot(grad_up, kind(j, 1), preferred_element_type=F32)
        kept = jnp.where(first, out, grad).astype(BF16)
        given = jnp.where(first, grad, out).astype(BF16)
        for i in range(n_rows):
            at = slice(i * capacity, (i + 1) * capacity)
            keep_ref, give_ref = out_refs[i]
            keep_ref[:, columns(j)] = kept[at]
            give_ref[:, columns(j)] = given[at]


def after(values, awaited):
    return lax.optimization_barrier((tuple(values), tuple(awaited)))[0]


def aligned_plan(tokens, cotangent, routes, cluster, w_gate, w_up, w_down):
    n_dp = lax.axis_size("dp")
    n_experts = lax.axis_size("expert")
    halves = lax.axis_size("tensor")
    shards = n_experts * halves
    width_part = w_gate.shape[1]
    tok_count, width = tokens.shape
    run = cluster.shape[1] // (halves * shards)
    per = halves * run
    capacity = 3 * tok_count // (2 * n_experts)
    params = pltpu.CompilerParams(vmem_limit_bytes=VMEM_LIMIT)
    vmem = pl.BlockSpec(memory_space=pltpu.VMEM)
    shape = jax.ShapeDtypeStruct

    sent_w = pl.pallas_call(
        functools.partial(select_kernel, n_experts, halves, shards),
        out_shape=[shape((3 * per, width_part), BF16)] * n_experts,
        in_specs=[pl.BlockSpec(memory_space=pltpu.HBM)] * 4,
        out_specs=[pl.BlockSpec(memory_space=pltpu.HBM)] * n_experts,
        scratch_shapes=[pltpu.VMEM(cluster.shape, jnp.int32)]
        + [pltpu.VMEM(w_gate.shape, BF16)] * 3
        + [
            pltpu.VMEM((3, n_experts * per, width_part), BF16),
            pltpu.SemaphoreType.DMA((4,)),
            pltpu.SemaphoreType.DMA((3, n_experts)),
        ],
        compiler_params=pltpu.CompilerParams(vmem_limit_bytes=MOST_VMEM),
        name="select_rows",
    )(cluster, w_gate, w_up, w_down)

    route_row = routes.reshape(1, tok_count)
    block = width // 4
    *sent, local, home_table = pl.pallas_call(
        functools.partial(dispatch_kernel, n_experts, capacity),
        grid=(width // block,),
        out_shape=[shape((capacity, width), BF16)] * (n_experts + 1)
        + [shape((tok_count, n_experts * capacity), BF16)],
        in_specs=[
            pl.BlockSpec((1, tok_count), lambda i: (0, 0)),
            pl.BlockSpec((tok_count, block), lambda i: (0, i)),
            pl.BlockSpec((tok_count, block), lambda i: (0, i)),
        ],
        out_specs=[pl.BlockSpec((capacity, block), lambda i: (0, i))] * (n_experts + 1)
        + [pl.BlockSpec((tok_count, n_experts * capacity), lambda i: (0, 0))],
        scratch_shapes=[pltpu.VMEM((n_experts * capacity, tok_count), BF16)],
        compiler_params=params,
        name="dispatch_rows",
    )(route_row, tokens, cotangent)

    swap = flips(halves, 1)

    def planes(chunk, k):
        return lax.ppermute(chunk, "expert", flips(n_experts, k))

    def spread(chunk, step):
        return lax.ppermute(chunk, "dp", flips(n_dp, step))

    def swapped(chunk):
        return lax.ppermute(chunk, "tensor", swap)

    def direct(chunk):
        return [chunk, spread(chunk, 1), spread(chunk, 2), spread(chunk, 3)]

    def near_far(chunk):
        return [chunk, spread(chunk, 1), spread(chunk, 2)]

    def diagonal(pieces):
        cut = pieces[0].shape[0] // 2
        return [spread(pieces[1][:cut], 2), spread(pieces[2][cut:], 1)]

    rows, others = {0: sent[0]}, {0: local}
    chunk3, chunk1 = planes(sent_w[3], 3), planes(sent_w[1], 1)
    pieces0 = direct(sent_w[0])
    (sent_w2,) = after([sent_w[2]], [chunk3])
    chunk2 = planes(sent_w2, 2)
    (chunk1,) = after([chunk1], pieces0[1:])
    pieces1 = near_far(chunk1)
    (chunk3,) = after([chunk3], [*pieces0[1:3], local])
    pieces3 = near_far(chunk3)
    (held,) = after([chunk2], pieces3[1:] + pieces1[1:])
    pieces2 = near_far(held)
    for k, awaited in ((2, chunk2), (1, chunk2), (3, None)):
        (row,) = after([sent[k]], [rows[2] if awaited is None else awaited])
        rows[k] = planes(row, k)
    pieces3.append(spread(pieces3[1], 2))
    pieces1.append(spread(pieces1[2], 1))
    held2 = after(pieces2[1:], [pieces1[3], pieces3[3]])
    pieces2 += diagonal([pieces2[0], *held2])
    for k in (2, 1, 3):
        others[k] = swapped(rows[k])

    weights = (pieces3, pieces2, pieces0, pieces1)
    mine, other, returned = {}, {}, []
    for members in ((2, 1), (3, 0)):
        count = len(members)
        here = {k: rows[k] for k in members}
        if returned:
            (here[3],) = after([rows[3]], returned[:1])
        out_shape = []
        for k in members:
            out_shape += [shape((capacity, width), BF16)] * 2 if k else [shape((2 * capacity, width), BF16)]
        results = pl.pallas_call(
            functools.partial(
                expert_kernel,
                [len(pieces) for pieces in weights],
                n_dp,
                count,
                members.index(0) if 0 in members else None,
            ),
            out_shape=out_shape,
            in_specs=[vmem] * (sum(len(pieces) for pieces in weights) + 2 * count),
            out_specs=[vmem] * len(out_shape),
            compiler_params=params,
            name="expert_math",
        )(
            *[piece for pieces in weights for piece in pieces],
            *[here[k] for k in members],
            *[others[k] for k in members],
        )
        results = list(results)
        for k in members:
            if not k:
                stayed = results.pop(0)
                stayed = (stayed, swapped(stayed))
                continue
            kept, given = results.pop(0), results.pop(0)
            total = (kept.astype(F32) + swapped(given).astype(F32)).astype(BF16)
            returned.append(total)
            mine[k] = planes(total, k)
    awaited = []
    for k in (2, 1, 3):
        other[k] = swapped(after([mine[k]], awaited)[0])
        awaited = [other[k]]

    order = (2, 1, 3)
    blocks = 8
    return tuple(
        pl.pallas_call(
            functools.partial(merge_kernel, order, capacity, blocks),
            out_shape=[shape((tok_count, width), BF16)] * 2,
            in_specs=[vmem] * (2 * n_experts + 1),
            out_specs=[pl.BlockSpec(memory_space=pltpu.HBM)] * 2,
            scratch_shapes=[
                pltpu.VMEM((2, tok_count, width), BF16),
                pltpu.SemaphoreType.DMA((2, blocks)),
            ],
            compiler_params=params,
            name="merge_rows",
        )(*[mine[k] for k in order], *[other[k] for k in order], *stayed, home_table)
    )


def expert_math(x_rows, dy_rows, gate_w, up_w, down_w):
    contract = (((1,), (1,)), ((), ()))
    pre_gate = lax.dot_general(x_rows, gate_w, contract, preferred_element_type=jnp.float32)
    pre_up = lax.dot_general(x_rows, up_w, contract, preferred_element_type=jnp.float32)
    sig_gate = jax.nn.sigmoid(pre_gate)
    hidden = (pre_gate * sig_gate * pre_up).astype(jnp.bfloat16)
    out_part = jnp.dot(hidden, down_w, preferred_element_type=jnp.float32)
    grad_hidden = lax.dot_general(dy_rows, down_w, contract, preferred_element_type=jnp.float32)
    grad_gate = (grad_hidden * pre_up * sig_gate * (1.0 + pre_gate * (1.0 - sig_gate))).astype(
        jnp.bfloat16
    )
    grad_up = (grad_hidden * pre_gate * sig_gate).astype(jnp.bfloat16)
    grad_part = jnp.dot(grad_gate, gate_w, preferred_element_type=jnp.float32)
    grad_part = grad_part + jnp.dot(grad_up, up_w, preferred_element_type=jnp.float32)
    return (out_part, grad_part)


def to_tokens(dispatch_table, returned):
    contract = (((0,), (0,)), ((), ()))
    merged = lax.dot_general(dispatch_table, returned, contract, preferred_element_type=jnp.float32)
    return merged.astype(jnp.bfloat16)


def general_plan(tokens, cotangent, routes, cluster, w_gate, w_up, w_down):
    shards = lax.axis_size(("expert", "tensor"))
    source = lax.axis_index(("expert", "tensor"))
    halves = lax.axis_size("tensor")
    rows_dev = w_gate.shape[0]
    width_part = w_gate.shape[1]
    n_experts = cluster.shape[0]
    half_slots = cluster.shape[1] // halves
    per_shard = half_slots // shards
    picks = cluster.reshape(shards, shards, per_shard)
    my_picks = lax.dynamic_index_in_dim(picks, source, 1, keepdims=False)
    is_live = (my_picks >= 0)[:, :, None]
    row_index = jnp.clip(my_picks - source * rows_dev, 0, rows_dev - 1).reshape(-1)

    def select_rows(weight):
        chosen = jnp.take(weight, row_index, axis=0).reshape(shards, per_shard, width_part)
        return jnp.where(is_live, chosen, jnp.zeros((), jnp.bfloat16))

    sent_gate = select_rows(w_gate)
    sent_up = select_rows(w_up)
    sent_down = select_rows(w_down)
    received = (
        lax.all_to_all(sent_gate, ("expert", "tensor"), split_axis=0, concat_axis=0, tiled=True),
        lax.all_to_all(sent_up, ("expert", "tensor"), split_axis=0, concat_axis=0, tiled=True),
        lax.all_to_all(sent_down, ("expert", "tensor"), split_axis=0, concat_axis=0, tiled=True),
    )
    part_gate = received[0].reshape(half_slots, width_part)
    part_up = received[1].reshape(half_slots, width_part)
    part_down = received[2].reshape(half_slots, width_part)
    gate_w, up_w, down_w = (
        lax.all_gather(part_gate, "dp", axis=1, tiled=True),
        lax.all_gather(part_up, "dp", axis=1, tiled=True),
        lax.all_gather(part_down, "dp", axis=1, tiled=True),
    )
    tok_count = tokens.shape[0]
    width = tokens.shape[1]
    capacity = max(2, 3 * tok_count // (2 * n_experts))
    expert_of = routes[:, 0]
    onehot = (expert_of[:, None] == jnp.arange(n_experts, dtype=jnp.int32)[None, :]).astype(
        jnp.int32
    )
    position = jnp.sum((jnp.cumsum(onehot, axis=0) - 1) * onehot, axis=1)
    slot_id = expert_of * capacity + position
    buffer_rows = n_experts * capacity
    dispatch_table = (slot_id[None, :] == jnp.arange(buffer_rows, dtype=jnp.int32)[:, None]).astype(
        jnp.bfloat16
    )
    sent_tokens = jnp.dot(dispatch_table, tokens, preferred_element_type=jnp.float32).astype(
        jnp.bfloat16
    )
    sent_grads = jnp.dot(dispatch_table, cotangent, preferred_element_type=jnp.float32).astype(
        jnp.bfloat16
    )
    sent_tokens = sent_tokens.reshape(n_experts, capacity, width)
    sent_grads = sent_grads.reshape(n_experts, capacity, width)
    x_rows, dy_rows = (
        lax.all_to_all(sent_tokens, "expert", split_axis=0, concat_axis=0, tiled=True),
        lax.all_to_all(sent_grads, "expert", split_axis=0, concat_axis=0, tiled=True),
    )
    x_rows = x_rows.reshape(buffer_rows, width)
    dy_rows = dy_rows.reshape(buffer_rows, width)
    out_part, grad_part = expert_math(x_rows, dy_rows, gate_w, up_w, down_w)
    out_total, grad_total = (
        lax.psum(out_part.astype(jnp.bfloat16), "tensor").astype(jnp.float32),
        lax.psum(grad_part.astype(jnp.bfloat16), "tensor").astype(jnp.float32),
    )
    out_back = out_total.astype(jnp.bfloat16).reshape(n_experts, capacity, width)
    grad_back = grad_total.astype(jnp.bfloat16).reshape(n_experts, capacity, width)
    out_home, grad_home = (
        lax.all_to_all(out_back, "expert", split_axis=0, concat_axis=0, tiled=True),
        lax.all_to_all(grad_back, "expert", split_axis=0, concat_axis=0, tiled=True),
    )
    layer_out = to_tokens(dispatch_table, out_home.reshape(buffer_rows, width))
    grad_out = to_tokens(dispatch_table, grad_home.reshape(buffer_rows, width))
    return (layer_out, grad_out)


def per_device(tokens, cotangent, routes, cluster, w_gate, w_up, w_down):
    n_experts = lax.axis_size("expert")
    halves = lax.axis_size("tensor")
    per = cluster.shape[1] // (halves * n_experts)
    capacity = 3 * tokens.shape[0] // (2 * n_experts)
    aligned = (
        per // halves % 16 == 0
        and capacity % 16 == 0
        and n_experts == 4
        and halves == 2
        and lax.axis_size("dp") == 4
    )
    plan = aligned_plan if aligned else general_plan
    return plan(tokens, cotangent, routes, cluster, w_gate, w_up, w_down)


def solution(mesh):
    in_specs = (
        P(("dp", "expert"), None),
        P(("dp", "expert"), None),
        P(("dp", "expert"), None),
        P(),
        P(("expert", "tensor"), "dp"),
        P(("expert", "tensor"), "dp"),
        P(("expert", "tensor"), "dp"),
    )
    out_specs = (P(("dp", "expert"), None), P(("dp", "expert"), None))
    return jax.shard_map(
        per_device, mesh=mesh, in_specs=in_specs, out_specs=out_specs, check_vma=False
    )
```

```python
import functools

import jax
import jax.numpy as jnp
from jax import lax
from jax.experimental import pallas as pl
from jax.experimental.pallas import tpu as pltpu
from jax.sharding import PartitionSpec as P

BF16 = jnp.bfloat16
F32 = jnp.float32
LAST = (((1,), (1,)), ((), ()))
VMEM_LIMIT = 16 * 1024 * 1024
MOST_VMEM = 60 * 1024 * 1024


def flips(size, step):
    return [(i, i ^ step) for i in range(size)]


def select_kernel(n_experts, halves, shards, cluster_hbm, gate_hbm, up_hbm, down_hbm, *refs):
    out_refs, scratch = refs[:n_experts], refs[n_experts:-3]
    chosen_ref, sems, out_sems = refs[-3:]
    sources = (cluster_hbm, gate_hbm, up_hbm, down_hbm)
    copies = [pltpu.make_async_copy(a, b, sems.at[i]) for i, (a, b) in enumerate(zip(sources, scratch))]
    for copy in copies:
        copy.start()
    cluster_ref, *weight_refs = scratch
    copies[0].wait()
    mine = lax.axis_index("expert")
    source = mine * halves + lax.axis_index("tensor")
    slots = cluster_ref.shape[1]
    rows = gate_hbm.shape[0]
    half = slots // halves
    run = half // shards
    wide = n_experts * halves * run
    lane = lax.broadcasted_iota(jnp.int32, (8, slots), 1)
    picks = jnp.full((8, slots), -1, jnp.int32)
    for k in range(n_experts):
        row = cluster_ref[pl.ds(mine ^ k, 1), :]
        row = jnp.broadcast_to(row, (8, slots))
        for q in range(halves):
            start = (k * halves + q) * run
            shift = lax.rem(start + 2 * slots - q * half - source * run, slots)
            moved = pltpu.roll(row, shift, 1)
            picks = jnp.where((lane >= start) & (lane < start + run), moved, picks)
    local = jnp.where(picks >= 0, picks - source * rows, -1)[0:1, :wide]
    down = jnp.transpose(jnp.broadcast_to(local, (wide, wide)))[:, :1]
    neuron = lax.broadcasted_iota(jnp.int32, (wide, rows), 1)
    table = jnp.where(neuron == down, 1.0, 0.0).astype(BF16)
    per = halves * run
    sent = []
    for w, ref in enumerate(weight_refs):
        copies[w + 1].wait()
        chosen_ref[w] = jnp.dot(table, ref[...], preferred_element_type=F32).astype(BF16)
        for k in range(n_experts):
            part, place = chosen_ref.at[w, pl.ds(k * per, per)], out_refs[k].at[pl.ds(w * per, per)]
            sent.append(pltpu.make_async_copy(part, place, out_sems.at[w, k]))
            sent[-1].start()
    for copy in sent:
        copy.wait()


def slot_table(routes, n_experts, capacity):
    tokens = routes.shape[1]
    across = jnp.broadcast_to(routes, (tokens, tokens))
    down = jnp.transpose(across)
    i = lax.broadcasted_iota(jnp.int32, (tokens, tokens), 0)
    j = lax.broadcasted_iota(jnp.int32, (tokens, tokens), 1)
    before = jnp.where((across == down) & (i < j), 1, 0)
    position = jnp.sum(before, axis=0, keepdims=True)
    slot = (routes ^ lax.axis_index("expert")) * capacity + position
    number = lax.broadcasted_iota(jnp.int32, (n_experts * capacity, tokens), 0)
    return jnp.where(number == slot, 1.0, 0.0)


def dispatch_kernel(n_experts, capacity, routes_ref, tokens_ref, cotangent_ref, *refs):
    out_refs, local_ref, home_ref, table_ref = refs[:n_experts], *refs[n_experts:]

    @pl.when(pl.program_id(0) == 0)
    def _():
        table = slot_table(routes_ref[...], n_experts, capacity)
        table_ref[...] = table.astype(BF16)
        home_ref[...] = jnp.transpose(table).astype(BF16)

    def rows(source_ref, count):
        return jnp.dot(table_ref[:count], source_ref[...], preferred_element_type=F32).astype(BF16)

    def send(mine_ref, other_ref):
        sent = rows(mine_ref, n_experts * capacity)
        for k in range(n_experts):
            out_refs[k][...] = sent[k * capacity:(k + 1) * capacity]
        local_ref[...] = rows(other_ref, capacity)

    core = lax.axis_index("tensor")
    pl.when(core == 0)(lambda: send(tokens_ref, cotangent_ref))
    pl.when(core != 0)(lambda: send(cotangent_ref, tokens_ref))


def merge_kernel(order, capacity, blocks, *refs):
    n_experts, count = len(order) + 1, len(order)
    mine_refs, other_refs = refs[:count], refs[count:2 * count]
    kept_ref, got_ref, table_ref, out_ref, grad_ref, held_ref, sems = refs[2 * count:]
    table = table_ref[...]
    width = out_ref.shape[1] // blocks
    first = lax.axis_index("tensor") == 0
    copies = []
    for i in range(blocks):
        at = pl.ds(i * width, width)

        def half(ref, h):
            return ref[h * capacity:(h + 1) * capacity, at].astype(F32)

        def rows(refs, h):
            parts = [refs[order.index(k)][:, at] for k in range(1, n_experts)]
            stayed = (half(kept_ref, h) + half(got_ref, 1 - h)).astype(BF16)
            return jnp.concatenate([stayed, *parts], axis=0)

        mine, other = rows(mine_refs, 0), rows(other_refs, 1)
        for w, (a, b, ref) in enumerate(((mine, other, out_ref), (other, mine, grad_ref))):
            total = jnp.dot(table, jnp.where(first, a, b), preferred_element_type=F32)
            held_ref[w, :, at] = total.astype(BF16)
            copies.append(pltpu.make_async_copy(held_ref.at[w, :, at], ref.at[:, at], sems.at[w, i]))
            copies[-1].start()
    for copy in copies:
        copy.wait()


def expert_kernel(n_parts, n_dp, n_rows, stacked, *refs):
    refs = list(refs)
    n_experts = len(n_parts)
    weights = [[refs.pop(0) for _ in range(count)] for count in n_parts]
    mine_refs = [refs.pop(0) for _ in range(n_rows)]
    other_refs = [refs.pop(0) for _ in range(n_rows)]
    capacity = mine_refs[0].shape[0]
    out_refs = []
    for i in range(n_rows):
        if i == stacked:
            ref = refs.pop(0)
            out_refs.append((ref.at[pl.ds(0, capacity)], ref.at[pl.ds(capacity, capacity)]))
        else:
            out_refs.append((refs.pop(0), refs.pop(0)))
    me = lax.axis_index("dp")
    first = lax.axis_index("tensor") == 0
    deep, width = weights[0][0].shape
    per, cut = deep // 3, deep // 2

    def columns(j):
        return pl.ds(pl.multiple_of((me ^ j) * width, width), width)

    def kind(j, w):
        parts = []
        lower, upper = w * per, (w + 1) * per
        for k in range(n_experts):
            if j < n_dp - 1 or n_parts[k] == n_dp:
                parts.append(weights[k][j][lower:upper, :])
                continue
            if lower < cut:
                parts.append(weights[k][j][lower:min(upper, cut), :])
            if upper > cut:
                parts.append(weights[k][j + 1][max(lower, cut) - cut:upper - cut, :])
        return jnp.concatenate(parts, axis=0)

    pre_gate = pre_up = grad_hidden = 0.0
    for j in range(n_dp):
        mine = jnp.concatenate([ref[:, columns(j)] for ref in mine_refs], axis=0)
        other = jnp.concatenate([ref[:, columns(j)] for ref in other_refs], axis=0)
        x = jnp.where(first, mine, other)
        dy = jnp.where(first, other, mine)
        pre_gate += lax.dot_general(x, kind(j, 0), LAST, preferred_element_type=F32)
        pre_up += lax.dot_general(x, kind(j, 1), LAST, preferred_element_type=F32)
        grad_hidden += lax.dot_general(dy, kind(j, 2), LAST, preferred_element_type=F32)
    sig = jax.nn.sigmoid(pre_gate)
    hidden = (pre_gate * sig * pre_up).astype(BF16)
    grad_gate = (grad_hidden * pre_up * sig * (1.0 + pre_gate * (1.0 - sig))).astype(BF16)
    grad_up = (grad_hidden * pre_gate * sig).astype(BF16)
    for j in range(n_dp):
        out = jnp.dot(hidden, kind(j, 2), preferred_element_type=F32)
        grad = jnp.dot(grad_gate, kind(j, 0), preferred_element_type=F32)
        grad = grad + jnp.dot(grad_up, kind(j, 1), preferred_element_type=F32)
        kept = jnp.where(first, out, grad).astype(BF16)
        given = jnp.where(first, grad, out).astype(BF16)
        for i in range(n_rows):
            at = slice(i * capacity, (i + 1) * capacity)
            keep_ref, give_ref = out_refs[i]
            keep_ref[:, columns(j)] = kept[at]
            give_ref[:, columns(j)] = given[at]


def after(values, awaited):
    return lax.optimization_barrier((tuple(values), tuple(awaited)))[0]


def aligned_plan(tokens, cotangent, routes, cluster, w_gate, w_up, w_down):
    n_dp = lax.axis_size("dp")
    n_experts = lax.axis_size("expert")
    halves = lax.axis_size("tensor")
    shards = n_experts * halves
    width_part = w_gate.shape[1]
    tok_count, width = tokens.shape
    run = cluster.shape[1] // (halves * shards)
    per = halves * run
    capacity = 3 * tok_count // (2 * n_experts)
    params = pltpu.CompilerParams(vmem_limit_bytes=VMEM_LIMIT)
    vmem = pl.BlockSpec(memory_space=pltpu.VMEM)
    shape = jax.ShapeDtypeStruct

    sent_w = pl.pallas_call(
        functools.partial(select_kernel, n_experts, halves, shards),
        out_shape=[shape((3 * per, width_part), BF16)] * n_experts,
        in_specs=[pl.BlockSpec(memory_space=pltpu.HBM)] * 4,
        out_specs=[pl.BlockSpec(memory_space=pltpu.HBM)] * n_experts,
        scratch_shapes=[pltpu.VMEM(cluster.shape, jnp.int32)]
        + [pltpu.VMEM(w_gate.shape, BF16)] * 3
        + [
            pltpu.VMEM((3, n_experts * per, width_part), BF16),
            pltpu.SemaphoreType.DMA((4,)),
            pltpu.SemaphoreType.DMA((3, n_experts)),
        ],
        compiler_params=pltpu.CompilerParams(vmem_limit_bytes=MOST_VMEM),
        name="select_rows",
    )(cluster, w_gate, w_up, w_down)

    route_row = routes.reshape(1, tok_count)
    block = width // 2
    *sent, local, home_table = pl.pallas_call(
        functools.partial(dispatch_kernel, n_experts, capacity),
        grid=(width // block,),
        out_shape=[shape((capacity, width), BF16)] * (n_experts + 1)
        + [shape((tok_count, n_experts * capacity), BF16)],
        in_specs=[
            pl.BlockSpec((1, tok_count), lambda i: (0, 0)),
            pl.BlockSpec((tok_count, block), lambda i: (0, i)),
            pl.BlockSpec((tok_count, block), lambda i: (0, i)),
        ],
        out_specs=[pl.BlockSpec((capacity, block), lambda i: (0, i))] * (n_experts + 1)
        + [pl.BlockSpec((tok_count, n_experts * capacity), lambda i: (0, 0))],
        scratch_shapes=[pltpu.VMEM((n_experts * capacity, tok_count), BF16)],
        compiler_params=params,
        name="dispatch_rows",
    )(route_row, tokens, cotangent)

    swap = flips(halves, 1)

    def planes(chunk, k):
        return lax.ppermute(chunk, "expert", flips(n_experts, k))

    def spread(chunk, step):
        return lax.ppermute(chunk, "dp", flips(n_dp, step))

    def swapped(chunk):
        return lax.ppermute(chunk, "tensor", swap)

    def direct(chunk):
        return [chunk, spread(chunk, 1), spread(chunk, 2), spread(chunk, 3)]

    def near_far(chunk):
        return [chunk, spread(chunk, 1), spread(chunk, 2)]

    def diagonal(pieces):
        cut = pieces[0].shape[0] // 2
        return [spread(pieces[1][:cut], 2), spread(pieces[2][cut:], 1)]

    rows, others = {0: sent[0]}, {0: local}
    chunk3, chunk1 = planes(sent_w[3], 3), planes(sent_w[1], 1)
    pieces0 = direct(sent_w[0])
    (sent_w2,) = after([sent_w[2]], [chunk3])
    chunk2 = planes(sent_w2, 2)
    (chunk1,) = after([chunk1], pieces0[1:])
    pieces1 = near_far(chunk1)
    (chunk3,) = after([chunk3], [*pieces0[1:3], local])
    pieces3 = near_far(chunk3)
    (held,) = after([chunk2], pieces3[2:3] + pieces1[1:2])
    pieces2 = near_far(held)
    for k, awaited in ((2, chunk2), (1, chunk2), (3, None)):
        (row,) = after([sent[k]], [rows[2] if awaited is None else awaited])
        rows[k] = planes(row, k)
    pieces3.append(spread(pieces3[1], 2))
    pieces1.append(spread(pieces1[2], 1))
    held2 = after(pieces2[1:], [pieces1[3], pieces3[3]])
    pieces2 += diagonal([pieces2[0], *held2])
    for k in (2, 1, 3):
        others[k] = swapped(rows[k])

    weights = (pieces3, pieces2, pieces0, pieces1)
    mine, other, returned = {}, {}, []
    for members in ((2, 1), (3, 0)):
        count = len(members)
        here = {k: rows[k] for k in members}
        if returned:
            (here[3],) = after([rows[3]], returned[:1])
        out_shape = []
        for k in members:
            out_shape += [shape((capacity, width), BF16)] * 2 if k else [shape((2 * capacity, width), BF16)]
        results = pl.pallas_call(
            functools.partial(
                expert_kernel,
                [len(pieces) for pieces in weights],
                n_dp,
                count,
                members.index(0) if 0 in members else None,
            ),
            out_shape=out_shape,
            in_specs=[vmem] * (sum(len(pieces) for pieces in weights) + 2 * count),
            out_specs=[vmem] * len(out_shape),
            compiler_params=params,
            name="expert_math",
        )(
            *[piece for pieces in weights for piece in pieces],
            *[here[k] for k in members],
            *[others[k] for k in members],
        )
        results = list(results)
        for k in members:
            if not k:
                stayed = results.pop(0)
                stayed = (stayed, swapped(stayed))
                continue
            kept, given = results.pop(0), results.pop(0)
            total = (kept.astype(F32) + swapped(given).astype(F32)).astype(BF16)
            returned.append(total)
            mine[k] = planes(total, k)
    awaited = []
    for k in (2, 1, 3):
        other[k] = swapped(after([mine[k]], awaited)[0])
        awaited = [other[k]]

    order = (2, 1, 3)
    blocks = 4
    return tuple(
        pl.pallas_call(
            functools.partial(merge_kernel, order, capacity, blocks),
            out_shape=[shape((tok_count, width), BF16)] * 2,
            in_specs=[vmem] * (2 * n_experts + 1),
            out_specs=[pl.BlockSpec(memory_space=pltpu.HBM)] * 2,
            scratch_shapes=[
                pltpu.VMEM((2, tok_count, width), BF16),
                pltpu.SemaphoreType.DMA((2, blocks)),
            ],
            compiler_params=params,
            name="merge_rows",
        )(*[mine[k] for k in order], *[other[k] for k in order], *stayed, home_table)
    )


def expert_math(x_rows, dy_rows, gate_w, up_w, down_w):
    contract = (((1,), (1,)), ((), ()))
    pre_gate = lax.dot_general(x_rows, gate_w, contract, preferred_element_type=jnp.float32)
    pre_up = lax.dot_general(x_rows, up_w, contract, preferred_element_type=jnp.float32)
    sig_gate = jax.nn.sigmoid(pre_gate)
    hidden = (pre_gate * sig_gate * pre_up).astype(jnp.bfloat16)
    out_part = jnp.dot(hidden, down_w, preferred_element_type=jnp.float32)
    grad_hidden = lax.dot_general(dy_rows, down_w, contract, preferred_element_type=jnp.float32)
    grad_gate = (grad_hidden * pre_up * sig_gate * (1.0 + pre_gate * (1.0 - sig_gate))).astype(
        jnp.bfloat16
    )
    grad_up = (grad_hidden * pre_gate * sig_gate).astype(jnp.bfloat16)
    grad_part = jnp.dot(grad_gate, gate_w, preferred_element_type=jnp.float32)
    grad_part = grad_part + jnp.dot(grad_up, up_w, preferred_element_type=jnp.float32)
    return (out_part, grad_part)


def to_tokens(dispatch_table, returned):
    contract = (((0,), (0,)), ((), ()))
    merged = lax.dot_general(dispatch_table, returned, contract, preferred_element_type=jnp.float32)
    return merged.astype(jnp.bfloat16)


def general_plan(tokens, cotangent, routes, cluster, w_gate, w_up, w_down):
    shards = lax.axis_size(("expert", "tensor"))
    source = lax.axis_index(("expert", "tensor"))
    halves = lax.axis_size("tensor")
    rows_dev = w_gate.shape[0]
    width_part = w_gate.shape[1]
    n_experts = cluster.shape[0]
    half_slots = cluster.shape[1] // halves
    per_shard = half_slots // shards
    picks = cluster.reshape(shards, shards, per_shard)
    my_picks = lax.dynamic_index_in_dim(picks, source, 1, keepdims=False)
    is_live = (my_picks >= 0)[:, :, None]
    row_index = jnp.clip(my_picks - source * rows_dev, 0, rows_dev - 1).reshape(-1)

    def select_rows(weight):
        chosen = jnp.take(weight, row_index, axis=0).reshape(shards, per_shard, width_part)
        return jnp.where(is_live, chosen, jnp.zeros((), jnp.bfloat16))

    sent_gate = select_rows(w_gate)
    sent_up = select_rows(w_up)
    sent_down = select_rows(w_down)
    received = (
        lax.all_to_all(sent_gate, ("expert", "tensor"), split_axis=0, concat_axis=0, tiled=True),
        lax.all_to_all(sent_up, ("expert", "tensor"), split_axis=0, concat_axis=0, tiled=True),
        lax.all_to_all(sent_down, ("expert", "tensor"), split_axis=0, concat_axis=0, tiled=True),
    )
    part_gate = received[0].reshape(half_slots, width_part)
    part_up = received[1].reshape(half_slots, width_part)
    part_down = received[2].reshape(half_slots, width_part)
    gate_w, up_w, down_w = (
        lax.all_gather(part_gate, "dp", axis=1, tiled=True),
        lax.all_gather(part_up, "dp", axis=1, tiled=True),
        lax.all_gather(part_down, "dp", axis=1, tiled=True),
    )
    tok_count = tokens.shape[0]
    width = tokens.shape[1]
    capacity = max(2, 3 * tok_count // (2 * n_experts))
    expert_of = routes[:, 0]
    onehot = (expert_of[:, None] == jnp.arange(n_experts, dtype=jnp.int32)[None, :]).astype(
        jnp.int32
    )
    position = jnp.sum((jnp.cumsum(onehot, axis=0) - 1) * onehot, axis=1)
    slot_id = expert_of * capacity + position
    buffer_rows = n_experts * capacity
    dispatch_table = (slot_id[None, :] == jnp.arange(buffer_rows, dtype=jnp.int32)[:, None]).astype(
        jnp.bfloat16
    )
    sent_tokens = jnp.dot(dispatch_table, tokens, preferred_element_type=jnp.float32).astype(
        jnp.bfloat16
    )
    sent_grads = jnp.dot(dispatch_table, cotangent, preferred_element_type=jnp.float32).astype(
        jnp.bfloat16
    )
    sent_tokens = sent_tokens.reshape(n_experts, capacity, width)
    sent_grads = sent_grads.reshape(n_experts, capacity, width)
    x_rows, dy_rows = (
        lax.all_to_all(sent_tokens, "expert", split_axis=0, concat_axis=0, tiled=True),
        lax.all_to_all(sent_grads, "expert", split_axis=0, concat_axis=0, tiled=True),
    )
    x_rows = x_rows.reshape(buffer_rows, width)
    dy_rows = dy_rows.reshape(buffer_rows, width)
    out_part, grad_part = expert_math(x_rows, dy_rows, gate_w, up_w, down_w)
    out_total, grad_total = (
        lax.psum(out_part.astype(jnp.bfloat16), "tensor").astype(jnp.float32),
        lax.psum(grad_part.astype(jnp.bfloat16), "tensor").astype(jnp.float32),
    )
    out_back = out_total.astype(jnp.bfloat16).reshape(n_experts, capacity, width)
    grad_back = grad_total.astype(jnp.bfloat16).reshape(n_experts, capacity, width)
    out_home, grad_home = (
        lax.all_to_all(out_back, "expert", split_axis=0, concat_axis=0, tiled=True),
        lax.all_to_all(grad_back, "expert", split_axis=0, concat_axis=0, tiled=True),
    )
    layer_out = to_tokens(dispatch_table, out_home.reshape(buffer_rows, width))
    grad_out = to_tokens(dispatch_table, grad_home.reshape(buffer_rows, width))
    return (layer_out, grad_out)


def per_device(tokens, cotangent, routes, cluster, w_gate, w_up, w_down):
    n_experts = lax.axis_size("expert")
    halves = lax.axis_size("tensor")
    per = cluster.shape[1] // (halves * n_experts)
    capacity = 3 * tokens.shape[0] // (2 * n_experts)
    aligned = (
        per // halves % 16 == 0
        and capacity % 16 == 0
        and n_experts == 4
        and halves == 2
        and lax.axis_size("dp") == 4
    )
    plan = aligned_plan if aligned else general_plan
    return plan(tokens, cotangent, routes, cluster, w_gate, w_up, w_down)


def solution(mesh):
    in_specs = (
        P(("dp", "expert"), None),
        P(("dp", "expert"), None),
        P(("dp", "expert"), None),
        P(),
        P(("expert", "tensor"), "dp"),
        P(("expert", "tensor"), "dp"),
        P(("expert", "tensor"), "dp"),
    )
    out_specs = (P(("dp", "expert"), None), P(("dp", "expert"), None))
    return jax.shard_map(
        per_device, mesh=mesh, in_specs=in_specs, out_specs=out_specs, check_vma=False
    )
```

```python
import functools

import jax
import jax.numpy as jnp
from jax import lax
from jax.experimental import pallas as pl
from jax.experimental.pallas import tpu as pltpu
from jax.sharding import PartitionSpec as P

BF16 = jnp.bfloat16
F32 = jnp.float32
LAST = (((1,), (1,)), ((), ()))
VMEM_LIMIT = 16 * 1024 * 1024
MOST_VMEM = 60 * 1024 * 1024


def flips(size, step):
    return [(i, i ^ step) for i in range(size)]


def select_kernel(n_experts, halves, shards, cluster_hbm, gate_hbm, up_hbm, down_hbm, *refs):
    out_refs, scratch = refs[:n_experts], refs[n_experts:-3]
    chosen_ref, sems, out_sems = refs[-3:]
    sources = (cluster_hbm, gate_hbm, up_hbm, down_hbm)
    copies = [pltpu.make_async_copy(a, b, sems.at[i]) for i, (a, b) in enumerate(zip(sources, scratch))]
    for copy in copies:
        copy.start()
    cluster_ref, *weight_refs = scratch
    copies[0].wait()
    mine = lax.axis_index("expert")
    source = mine * halves + lax.axis_index("tensor")
    slots = cluster_ref.shape[1]
    rows = gate_hbm.shape[0]
    half = slots // halves
    run = half // shards
    wide = n_experts * halves * run
    lane = lax.broadcasted_iota(jnp.int32, (8, slots), 1)
    picks = jnp.full((8, slots), -1, jnp.int32)
    for k in range(n_experts):
        row = cluster_ref[pl.ds(mine ^ k, 1), :]
        row = jnp.broadcast_to(row, (8, slots))
        for q in range(halves):
            start = (k * halves + q) * run
            shift = lax.rem(start + 2 * slots - q * half - source * run, slots)
            moved = pltpu.roll(row, shift, 1)
            picks = jnp.where((lane >= start) & (lane < start + run), moved, picks)
    local = jnp.where(picks >= 0, picks - source * rows, -1)[0:1, :wide]
    down = jnp.transpose(jnp.broadcast_to(local, (wide, wide)))[:, :1]
    neuron = lax.broadcasted_iota(jnp.int32, (wide, rows), 1)
    table = jnp.where(neuron == down, 1.0, 0.0).astype(BF16)
    per = halves * run
    sent = []
    for w, ref in enumerate(weight_refs):
        copies[w + 1].wait()
        chosen_ref[w] = jnp.dot(table, ref[...], preferred_element_type=F32).astype(BF16)
        for k in range(n_experts):
            part, place = chosen_ref.at[w, pl.ds(k * per, per)], out_refs[k].at[pl.ds(w * per, per)]
            sent.append(pltpu.make_async_copy(part, place, out_sems.at[w, k]))
            sent[-1].start()
    for copy in sent:
        copy.wait()


def slot_table(routes, n_experts, capacity):
    tokens = routes.shape[1]
    across = jnp.broadcast_to(routes, (tokens, tokens))
    down = jnp.transpose(across)
    i = lax.broadcasted_iota(jnp.int32, (tokens, tokens), 0)
    j = lax.broadcasted_iota(jnp.int32, (tokens, tokens), 1)
    before = jnp.where((across == down) & (i < j), 1, 0)
    position = jnp.sum(before, axis=0, keepdims=True)
    slot = (routes ^ lax.axis_index("expert")) * capacity + position
    number = lax.broadcasted_iota(jnp.int32, (n_experts * capacity, tokens), 0)
    return jnp.where(number == slot, 1.0, 0.0)


def dispatch_kernel(n_experts, capacity, routes_ref, tokens_ref, cotangent_ref, *refs):
    out_refs, local_ref, home_ref, table_ref = refs[:n_experts], *refs[n_experts:]

    @pl.when(pl.program_id(0) == 0)
    def _():
        table = slot_table(routes_ref[...], n_experts, capacity)
        table_ref[...] = table.astype(BF16)
        home_ref[...] = jnp.transpose(table).astype(BF16)

    def rows(source_ref, count):
        return jnp.dot(table_ref[:count], source_ref[...], preferred_element_type=F32).astype(BF16)

    def send(mine_ref, other_ref):
        sent = rows(mine_ref, n_experts * capacity)
        for k in range(n_experts):
            out_refs[k][...] = sent[k * capacity:(k + 1) * capacity]
        local_ref[...] = rows(other_ref, capacity)

    core = lax.axis_index("tensor")
    pl.when(core == 0)(lambda: send(tokens_ref, cotangent_ref))
    pl.when(core != 0)(lambda: send(cotangent_ref, tokens_ref))


def merge_kernel(order, capacity, blocks, *refs):
    n_experts, count = len(order) + 1, len(order)
    mine_refs, other_refs = refs[:count], refs[count:2 * count]
    kept_ref, got_ref, table_ref, out_ref, grad_ref, held_ref, sems = refs[2 * count:]
    table = table_ref[...]
    width = out_ref.shape[1] // blocks
    first = lax.axis_index("tensor") == 0
    copies = []
    for i in range(blocks):
        at = pl.ds(i * width, width)

        def half(ref, h):
            return ref[h * capacity:(h + 1) * capacity, at].astype(F32)

        def rows(refs, h):
            parts = [refs[order.index(k)][:, at] for k in range(1, n_experts)]
            stayed = (half(kept_ref, h) + half(got_ref, 1 - h)).astype(BF16)
            return jnp.concatenate([stayed, *parts], axis=0)

        mine, other = rows(mine_refs, 0), rows(other_refs, 1)
        for w, (a, b, ref) in enumerate(((mine, other, out_ref), (other, mine, grad_ref))):
            total = jnp.dot(table, jnp.where(first, a, b), preferred_element_type=F32)
            held_ref[w, :, at] = total.astype(BF16)
            copies.append(pltpu.make_async_copy(held_ref.at[w, :, at], ref.at[:, at], sems.at[w, i]))
            copies[-1].start()
    for copy in copies:
        copy.wait()


def expert_kernel(n_parts, n_dp, n_rows, stacked, *refs):
    refs = list(refs)
    n_experts = len(n_parts)
    weights = [[refs.pop(0) for _ in range(count)] for count in n_parts]
    mine_refs = [refs.pop(0) for _ in range(n_rows)]
    other_refs = [refs.pop(0) for _ in range(n_rows)]
    capacity = mine_refs[0].shape[0]
    out_refs = []
    for i in range(n_rows):
        if i == stacked:
            ref = refs.pop(0)
            out_refs.append((ref.at[pl.ds(0, capacity)], ref.at[pl.ds(capacity, capacity)]))
        else:
            out_refs.append((refs.pop(0), refs.pop(0)))
    me = lax.axis_index("dp")
    first = lax.axis_index("tensor") == 0
    deep, width = weights[0][0].shape
    per, cut = deep // 3, deep // 2

    def columns(j):
        return pl.ds(pl.multiple_of((me ^ j) * width, width), width)

    def kind(j, w):
        parts = []
        lower, upper = w * per, (w + 1) * per
        for k in range(n_experts):
            if j < n_dp - 1 or n_parts[k] == n_dp:
                parts.append(weights[k][j][lower:upper, :])
                continue
            if lower < cut:
                parts.append(weights[k][j][lower:min(upper, cut), :])
            if upper > cut:
                parts.append(weights[k][j + 1][max(lower, cut) - cut:upper - cut, :])
        return jnp.concatenate(parts, axis=0)

    pre_gate = pre_up = grad_hidden = 0.0
    for j in range(n_dp):
        mine = jnp.concatenate([ref[:, columns(j)] for ref in mine_refs], axis=0)
        other = jnp.concatenate([ref[:, columns(j)] for ref in other_refs], axis=0)
        x = jnp.where(first, mine, other)
        dy = jnp.where(first, other, mine)
        pre_gate += lax.dot_general(x, kind(j, 0), LAST, preferred_element_type=F32)
        pre_up += lax.dot_general(x, kind(j, 1), LAST, preferred_element_type=F32)
        grad_hidden += lax.dot_general(dy, kind(j, 2), LAST, preferred_element_type=F32)
    sig = jax.nn.sigmoid(pre_gate)
    hidden = (pre_gate * sig * pre_up).astype(BF16)
    grad_gate = (grad_hidden * pre_up * sig * (1.0 + pre_gate * (1.0 - sig))).astype(BF16)
    grad_up = (grad_hidden * pre_gate * sig).astype(BF16)
    for j in range(n_dp):
        out = jnp.dot(hidden, kind(j, 2), preferred_element_type=F32)
        grad = jnp.dot(grad_gate, kind(j, 0), preferred_element_type=F32)
        grad = grad + jnp.dot(grad_up, kind(j, 1), preferred_element_type=F32)
        kept = jnp.where(first, out, grad).astype(BF16)
        given = jnp.where(first, grad, out).astype(BF16)
        for i in range(n_rows):
            at = slice(i * capacity, (i + 1) * capacity)
            keep_ref, give_ref = out_refs[i]
            keep_ref[:, columns(j)] = kept[at]
            give_ref[:, columns(j)] = given[at]


def after(values, awaited):
    return lax.optimization_barrier((tuple(values), tuple(awaited)))[0]


def aligned_plan(tokens, cotangent, routes, cluster, w_gate, w_up, w_down):
    n_dp = lax.axis_size("dp")
    n_experts = lax.axis_size("expert")
    halves = lax.axis_size("tensor")
    shards = n_experts * halves
    width_part = w_gate.shape[1]
    tok_count, width = tokens.shape
    run = cluster.shape[1] // (halves * shards)
    per = halves * run
    capacity = 3 * tok_count // (2 * n_experts)
    params = pltpu.CompilerParams(vmem_limit_bytes=VMEM_LIMIT)
    vmem = pl.BlockSpec(memory_space=pltpu.VMEM)
    shape = jax.ShapeDtypeStruct

    sent_w = pl.pallas_call(
        functools.partial(select_kernel, n_experts, halves, shards),
        out_shape=[shape((3 * per, width_part), BF16)] * n_experts,
        in_specs=[pl.BlockSpec(memory_space=pltpu.HBM)] * 4,
        out_specs=[pl.BlockSpec(memory_space=pltpu.HBM)] * n_experts,
        scratch_shapes=[pltpu.VMEM(cluster.shape, jnp.int32)]
        + [pltpu.VMEM(w_gate.shape, BF16)] * 3
        + [
            pltpu.VMEM((3, n_experts * per, width_part), BF16),
            pltpu.SemaphoreType.DMA((4,)),
            pltpu.SemaphoreType.DMA((3, n_experts)),
        ],
        compiler_params=pltpu.CompilerParams(vmem_limit_bytes=MOST_VMEM),
        name="select_rows",
    )(cluster, w_gate, w_up, w_down)

    route_row = routes.reshape(1, tok_count)
    block = width // 2
    *sent, local, home_table = pl.pallas_call(
        functools.partial(dispatch_kernel, n_experts, capacity),
        grid=(width // block,),
        out_shape=[shape((capacity, width), BF16)] * (n_experts + 1)
        + [shape((tok_count, n_experts * capacity), BF16)],
        in_specs=[
            pl.BlockSpec((1, tok_count), lambda i: (0, 0)),
            pl.BlockSpec((tok_count, block), lambda i: (0, i)),
            pl.BlockSpec((tok_count, block), lambda i: (0, i)),
        ],
        out_specs=[pl.BlockSpec((capacity, block), lambda i: (0, i))] * (n_experts + 1)
        + [pl.BlockSpec((tok_count, n_experts * capacity), lambda i: (0, 0))],
        scratch_shapes=[pltpu.VMEM((n_experts * capacity, tok_count), BF16)],
        compiler_params=params,
        name="dispatch_rows",
    )(route_row, tokens, cotangent)

    swap = flips(halves, 1)

    def planes(chunk, k):
        return lax.ppermute(chunk, "expert", flips(n_experts, k))

    def spread(chunk, step):
        return lax.ppermute(chunk, "dp", flips(n_dp, step))

    def swapped(chunk):
        return lax.ppermute(chunk, "tensor", swap)

    def direct(chunk):
        return [chunk, spread(chunk, 1), spread(chunk, 2), spread(chunk, 3)]

    def near_far(chunk):
        return [chunk, spread(chunk, 1), spread(chunk, 2)]

    def diagonal(pieces):
        cut = pieces[0].shape[0] // 2
        return [spread(pieces[1][:cut], 2), spread(pieces[2][cut:], 1)]

    rows, others = {0: sent[0]}, {0: local}
    chunk3, chunk1 = planes(sent_w[3], 3), planes(sent_w[1], 1)
    pieces0 = direct(sent_w[0])
    (sent_w2,) = after([sent_w[2]], [chunk3])
    chunk2 = planes(sent_w2, 2)
    (chunk1,) = after([chunk1], pieces0[1:])
    pieces1 = near_far(chunk1)
    (chunk3,) = after([chunk3], [*pieces0[1:3], local])
    pieces3 = near_far(chunk3)
    (held,) = after([chunk2], pieces3[2:3] + pieces1[1:2])
    pieces2 = near_far(held)
    for k, awaited in ((2, chunk2), (1, chunk2), (3, None)):
        (row,) = after([sent[k]], [rows[2] if awaited is None else awaited])
        rows[k] = planes(row, k)
    pieces3.append(spread(pieces3[1], 2))
    pieces1.append(spread(pieces1[2], 1))
    held2 = after(pieces2[1:], [pieces1[3], pieces3[3]])
    pieces2 += diagonal([pieces2[0], *held2])
    for k in (2, 1, 3):
        others[k] = swapped(rows[k])

    weights = (pieces3, pieces2, pieces0, pieces1)
    mine, other, returned = {}, {}, []
    for members in ((2, 1), (3, 0)):
        count = len(members)
        here = {k: rows[k] for k in members}
        if returned:
            (here[3],) = after([rows[3]], returned[:1])
        out_shape = []
        for k in members:
            out_shape += [shape((capacity, width), BF16)] * 2 if k else [shape((2 * capacity, width), BF16)]
        results = pl.pallas_call(
            functools.partial(
                expert_kernel,
                [len(pieces) for pieces in weights],
                n_dp,
                count,
                members.index(0) if 0 in members else None,
            ),
            out_shape=out_shape,
            in_specs=[vmem] * (sum(len(pieces) for pieces in weights) + 2 * count),
            out_specs=[vmem] * len(out_shape),
            compiler_params=params,
            name="expert_math",
        )(
            *[piece for pieces in weights for piece in pieces],
            *[here[k] for k in members],
            *[others[k] for k in members],
        )
        results = list(results)
        for k in members:
            if not k:
                stayed = results.pop(0)
                stayed = (stayed, swapped(stayed))
                continue
            kept, given = results.pop(0), results.pop(0)
            total = (kept.astype(F32) + swapped(given).astype(F32)).astype(BF16)
            returned.append(total)
            mine[k] = planes(total, k)
    awaited = []
    for k in (2, 1, 3):
        other[k] = swapped(after([mine[k]], awaited)[0])
        awaited = [other[k]]

    order = (2, 1, 3)
    blocks = 16
    return tuple(
        pl.pallas_call(
            functools.partial(merge_kernel, order, capacity, blocks),
            out_shape=[shape((tok_count, width), BF16)] * 2,
            in_specs=[vmem] * (2 * n_experts + 1),
            out_specs=[pl.BlockSpec(memory_space=pltpu.HBM)] * 2,
            scratch_shapes=[
                pltpu.VMEM((2, tok_count, width), BF16),
                pltpu.SemaphoreType.DMA((2, blocks)),
            ],
            compiler_params=params,
            name="merge_rows",
        )(*[mine[k] for k in order], *[other[k] for k in order], *stayed, home_table)
    )


def expert_math(x_rows, dy_rows, gate_w, up_w, down_w):
    contract = (((1,), (1,)), ((), ()))
    pre_gate = lax.dot_general(x_rows, gate_w, contract, preferred_element_type=jnp.float32)
    pre_up = lax.dot_general(x_rows, up_w, contract, preferred_element_type=jnp.float32)
    sig_gate = jax.nn.sigmoid(pre_gate)
    hidden = (pre_gate * sig_gate * pre_up).astype(jnp.bfloat16)
    out_part = jnp.dot(hidden, down_w, preferred_element_type=jnp.float32)
    grad_hidden = lax.dot_general(dy_rows, down_w, contract, preferred_element_type=jnp.float32)
    grad_gate = (grad_hidden * pre_up * sig_gate * (1.0 + pre_gate * (1.0 - sig_gate))).astype(
        jnp.bfloat16
    )
    grad_up = (grad_hidden * pre_gate * sig_gate).astype(jnp.bfloat16)
    grad_part = jnp.dot(grad_gate, gate_w, preferred_element_type=jnp.float32)
    grad_part = grad_part + jnp.dot(grad_up, up_w, preferred_element_type=jnp.float32)
    return (out_part, grad_part)


def to_tokens(dispatch_table, returned):
    contract = (((0,), (0,)), ((), ()))
    merged = lax.dot_general(dispatch_table, returned, contract, preferred_element_type=jnp.float32)
    return merged.astype(jnp.bfloat16)


def general_plan(tokens, cotangent, routes, cluster, w_gate, w_up, w_down):
    shards = lax.axis_size(("expert", "tensor"))
    source = lax.axis_index(("expert", "tensor"))
    halves = lax.axis_size("tensor")
    rows_dev = w_gate.shape[0]
    width_part = w_gate.shape[1]
    n_experts = cluster.shape[0]
    half_slots = cluster.shape[1] // halves
    per_shard = half_slots // shards
    picks = cluster.reshape(shards, shards, per_shard)
    my_picks = lax.dynamic_index_in_dim(picks, source, 1, keepdims=False)
    is_live = (my_picks >= 0)[:, :, None]
    row_index = jnp.clip(my_picks - source * rows_dev, 0, rows_dev - 1).reshape(-1)

    def select_rows(weight):
        chosen = jnp.take(weight, row_index, axis=0).reshape(shards, per_shard, width_part)
        return jnp.where(is_live, chosen, jnp.zeros((), jnp.bfloat16))

    sent_gate = select_rows(w_gate)
    sent_up = select_rows(w_up)
    sent_down = select_rows(w_down)
    received = (
        lax.all_to_all(sent_gate, ("expert", "tensor"), split_axis=0, concat_axis=0, tiled=True),
        lax.all_to_all(sent_up, ("expert", "tensor"), split_axis=0, concat_axis=0, tiled=True),
        lax.all_to_all(sent_down, ("expert", "tensor"), split_axis=0, concat_axis=0, tiled=True),
    )
    part_gate = received[0].reshape(half_slots, width_part)
    part_up = received[1].reshape(half_slots, width_part)
    part_down = received[2].reshape(half_slots, width_part)
    gate_w, up_w, down_w = (
        lax.all_gather(part_gate, "dp", axis=1, tiled=True),
        lax.all_gather(part_up, "dp", axis=1, tiled=True),
        lax.all_gather(part_down, "dp", axis=1, tiled=True),
    )
    tok_count = tokens.shape[0]
    width = tokens.shape[1]
    capacity = max(2, 3 * tok_count // (2 * n_experts))
    expert_of = routes[:, 0]
    onehot = (expert_of[:, None] == jnp.arange(n_experts, dtype=jnp.int32)[None, :]).astype(
        jnp.int32
    )
    position = jnp.sum((jnp.cumsum(onehot, axis=0) - 1) * onehot, axis=1)
    slot_id = expert_of * capacity + position
    buffer_rows = n_experts * capacity
    dispatch_table = (slot_id[None, :] == jnp.arange(buffer_rows, dtype=jnp.int32)[:, None]).astype(
        jnp.bfloat16
    )
    sent_tokens = jnp.dot(dispatch_table, tokens, preferred_element_type=jnp.float32).astype(
        jnp.bfloat16
    )
    sent_grads = jnp.dot(dispatch_table, cotangent, preferred_element_type=jnp.float32).astype(
        jnp.bfloat16
    )
    sent_tokens = sent_tokens.reshape(n_experts, capacity, width)
    sent_grads = sent_grads.reshape(n_experts, capacity, width)
    x_rows, dy_rows = (
        lax.all_to_all(sent_tokens, "expert", split_axis=0, concat_axis=0, tiled=True),
        lax.all_to_all(sent_grads, "expert", split_axis=0, concat_axis=0, tiled=True),
    )
    x_rows = x_rows.reshape(buffer_rows, width)
    dy_rows = dy_rows.reshape(buffer_rows, width)
    out_part, grad_part = expert_math(x_rows, dy_rows, gate_w, up_w, down_w)
    out_total, grad_total = (
        lax.psum(out_part.astype(jnp.bfloat16), "tensor").astype(jnp.float32),
        lax.psum(grad_part.astype(jnp.bfloat16), "tensor").astype(jnp.float32),
    )
    out_back = out_total.astype(jnp.bfloat16).reshape(n_experts, capacity, width)
    grad_back = grad_total.astype(jnp.bfloat16).reshape(n_experts, capacity, width)
    out_home, grad_home = (
        lax.all_to_all(out_back, "expert", split_axis=0, concat_axis=0, tiled=True),
        lax.all_to_all(grad_back, "expert", split_axis=0, concat_axis=0, tiled=True),
    )
    layer_out = to_tokens(dispatch_table, out_home.reshape(buffer_rows, width))
    grad_out = to_tokens(dispatch_table, grad_home.reshape(buffer_rows, width))
    return (layer_out, grad_out)


def per_device(tokens, cotangent, routes, cluster, w_gate, w_up, w_down):
    n_experts = lax.axis_size("expert")
    halves = lax.axis_size("tensor")
    per = cluster.shape[1] // (halves * n_experts)
    capacity = 3 * tokens.shape[0] // (2 * n_experts)
    aligned = (
        per // halves % 16 == 0
        and capacity % 16 == 0
        and n_experts == 4
        and halves == 2
        and lax.axis_size("dp") == 4
    )
    plan = aligned_plan if aligned else general_plan
    return plan(tokens, cotangent, routes, cluster, w_gate, w_up, w_down)


def solution(mesh):
    in_specs = (
        P(("dp", "expert"), None),
        P(("dp", "expert"), None),
        P(("dp", "expert"), None),
        P(),
        P(("expert", "tensor"), "dp"),
        P(("expert", "tensor"), "dp"),
        P(("expert", "tensor"), "dp"),
    )
    out_specs = (P(("dp", "expert"), None), P(("dp", "expert"), None))
    return jax.shard_map(
        per_device, mesh=mesh, in_specs=in_specs, out_specs=out_specs, check_vma=False
    )
```
